512 devices in a mesh: space: 32 (over x, z_hi, core), dp: 16 (over y, z_lo).
Axes of the slice: x: 4, y: 4, z: 16 (z_hi: 4, z_lo: 4; z = z_hi * 4 + z_lo), core: 2. Of those that a mesh axis runs over, the one named last changes fastest.
Arguments:
- tokens: bfloat16 [294912, 512], P(('space', 'dp')), may hold values from -6 to 6
- gain: float32 [512], replicated, may hold values from 0.25 to 1.75
- w_in: bfloat16 [32, 512, 1024], P('space'), may hold values from -0.25 to 0.25
- w_out: bfloat16 [32, 1024, 512], P('space'), may hold values from -0.1875 to 0.1875
- expert_ids: int32 [294912, 1], P(('space', 'dp')), may hold values from 0 to 31
- gate: bfloat16 [294912], P(('space', 'dp')), may hold values from 0.25 to 1
- grad_out: bfloat16 [294912, 512], P(('space', 'dp')), may hold values from -6 to 6
Outputs:
- grad_tokens: bfloat16 [294912, 512], P(('space', 'dp'))
- grad_gate: bfloat16 [294912], P(('space', 'dp'))
- grad_w_in: float32 [32, 512, 1024], P('space', 'dp')
- grad_w_out: float32 [32, 1024, 512], P('space', 'dp')
The draws below stay inside these ranges and needn't reach their ends.
All inputs are finite; a program needn't handle non-finite values.
Results may differ from the reference program's by a relative error of at most 0.02.
Values may be sent and summed in bfloat16 or wider, within the bound.
A program may use at most 64 MiB of HBM per device.

```python
import jax
import jax.numpy as jnp
from jax import lax

D = 512
FF = 1024
TOK_DEV = 576
EXPERTS = 32
CAP = 24
TOKENS = 294912
N_SPACE = 32
N_DP = 16


def level_of(key, dims, split, smallest, high):
    level = 1.0
    for position, parts in split:
        draws = jax.random.uniform(jax.random.fold_in(jax.random.fold_in(key, 6), position), (parts,), jnp.float32, smallest / len(split), high / len(split))
        level = level * jnp.repeat(jnp.exp(draws), dims[position] // parts).reshape((-1,) + (1,) * (len(dims) - 1 - position))
    return level


def choose_distinct(own_key, rows, count, top, lift):
    sequence = jax.random.permutation(jax.random.fold_in(own_key, 1), count)
    favour = sequence
    for power in range(3):
        favour = favour * favour // count
    favour = favour * lift // count
    chance = jax.random.randint(jax.random.fold_in(own_key, 2), (rows, count), 0, 4096) + favour
    sure = jax.random.permutation(jax.random.fold_in(own_key, 3), rows)[jnp.arange(count) % rows]
    chance = jnp.where(jnp.arange(rows)[:, None] == sure[None, :], 1 << 14, chance)
    merit = chance * count + jnp.arange(count)
    return lax.top_k(merit.astype(jnp.int32), top)[1].astype(jnp.int32)


def normal_values(key, extent, deviation, bound, shards=(), kind=jnp.bfloat16):
    factor_of = level_of(key, extent, shards, -0.22, 0.18) if shards else 1.0
    values = jax.random.normal(key, extent, jnp.float32) * deviation * factor_of
    return jnp.minimum(jnp.maximum(values, -bound), bound).astype(kind)


def setup_inputs(seed: int = 0) -> dict:
    arg_keys = jax.random.split(jax.random.key(seed), 8)
    tokens = normal_values(arg_keys[0], (TOKENS, D), 1.0, 6.0, ((0, 512),))
    gain = jnp.clip(1.0 + 0.15 * jax.random.normal(arg_keys[1], (D,), jnp.float32), 0.25, 1.75)
    w_in = normal_values(arg_keys[2], (EXPERTS, D, FF), D ** -0.5, 0.25, ((0, 32),))
    w_out = normal_values(arg_keys[3], (EXPERTS, FF, D), FF ** -0.5, 0.1875, ((0, 32),))
    expert_ids = choose_distinct(arg_keys[4], TOKENS, EXPERTS, 1, 256)
    gate = jnp.clip(0.25 + 0.75 * jax.random.uniform(arg_keys[5], (TOKENS,), jnp.float32) ** level_of(arg_keys[5], (TOKENS,), ((0, 512),), -0.2, 0.2), 0.25, 1.0).astype(jnp.bfloat16)
    grad_out = normal_values(arg_keys[6], (TOKENS, D), 1.0, 6.0, ((0, 512),))
    return dict(tokens=tokens, gain=gain, w_in=w_in, w_out=w_out, expert_ids=expert_ids, gate=gate, grad_out=grad_out)


epsilon = 1e-05

def normalize(tokens, gain):
    values = tokens.astype(jnp.float32)
    center = values - lax.optimization_barrier(jnp.mean(values, axis=-1, keepdims=True))
    spread = lax.rsqrt(lax.optimization_barrier(jnp.mean(center * center, axis=-1, keepdims=True)) + epsilon)
    scaled = center * spread
    return (scaled, spread, (scaled * gain).astype(jnp.bfloat16))

def slot_ranks(routes, experts):
    onehot = (routes[:, None] == jnp.arange(experts, dtype=jnp.int32)[None, :]).astype(jnp.int32)
    before = jnp.cumsum(onehot, axis=0) - onehot
    return lax.optimization_barrier(jnp.sum(before * onehot, axis=1)).astype(jnp.int32)

def norm_backward(grad_norm, scaled, spread, gain):
    scaled_grad = grad_norm.astype(jnp.float32) * gain
    grad_mean = lax.optimization_barrier(jnp.mean(scaled_grad, axis=-1, keepdims=True))
    grad_cross = lax.optimization_barrier(jnp.mean(scaled_grad * scaled, axis=-1, keepdims=True))
    return spread * (scaled_grad - grad_mean - scaled * grad_cross)

def place_rows(rows, target):
    blank_rows = jnp.zeros((EXPERTS * CAP, D), rows.dtype)
    return blank_rows.at[target].set(rows, mode='drop')

def expert_work(operands):
    normed_rows, delta_rows, weight_in, weight_out = operands
    preact = jnp.einsum('grd,df->grf', normed_rows.astype(jnp.float32), weight_in.astype(jnp.float32))
    act_float, gelu_back = jax.vjp(jax.nn.gelu, preact)
    activity = act_float.astype(jnp.bfloat16)
    token_out = jnp.einsum('grf,fd->grd', activity.astype(jnp.float32), weight_out.astype(jnp.float32)).astype(jnp.bfloat16)
    grad_activity = jnp.einsum('grd,fd->grf', delta_rows.astype(jnp.float32), weight_out.astype(jnp.float32))
    grad_preact = gelu_back(grad_activity)[0].astype(jnp.bfloat16)
    grad_normed = jnp.einsum('grf,df->grd', grad_preact.astype(jnp.float32), weight_in.astype(jnp.float32)).astype(jnp.bfloat16)
    part_in = jnp.einsum('grd,grf->gdf', normed_rows.astype(jnp.float32), grad_preact.astype(jnp.float32)).astype(jnp.bfloat16)
    part_out = jnp.einsum('grf,grd->gfd', activity.astype(jnp.float32), delta_rows.astype(jnp.float32)).astype(jnp.bfloat16)
    sum_in = lax.optimization_barrier(jnp.sum(lax.optimization_barrier(part_in).astype(jnp.float32), axis=0))
    sum_out = lax.optimization_barrier(jnp.sum(lax.optimization_barrier(part_out).astype(jnp.float32), axis=0))
    return (token_out, grad_normed, sum_in, sum_out)

def reference(tokens, gain, w_in, w_out, expert_ids, gate, grad_out):
    blocks = (N_SPACE, N_DP, TOK_DEV)
    scaled, spread, normed = normalize(tokens.reshape(blocks + (D,)), gain)
    routes = expert_ids.reshape(blocks)
    slot_rank = jax.vmap(jax.vmap(lambda routed: slot_ranks(routed, EXPERTS)))(routes)
    kept_mask = slot_rank < CAP
    target = jnp.where(kept_mask, routes * CAP + slot_rank, EXPERTS * CAP).astype(jnp.int32)
    grad_float = grad_out.reshape(blocks + (D,)).astype(jnp.float32)
    gate_float = gate.reshape(blocks).astype(jnp.float32)
    delta = (gate_float[..., None] * grad_float).astype(jnp.bfloat16)
    placer = jax.vmap(jax.vmap(place_rows))

    def to_experts(rows):
        placed = placer(rows, target).reshape(N_SPACE, N_DP, EXPERTS, CAP, D)
        return placed.transpose(2, 1, 0, 3, 4).reshape(EXPERTS, N_DP, N_SPACE * CAP, D)

    def to_tokens(rows):
        back = rows.reshape(EXPERTS, N_DP, N_SPACE, CAP, D).transpose(2, 1, 0, 3, 4)
        back = back.reshape(N_SPACE, N_DP, EXPERTS * CAP, D)
        row_index = jnp.minimum(target, EXPERTS * CAP - 1)
        return jnp.take_along_axis(back, row_index[..., None], axis=2)
    outputs, grads, grad_w_in, grad_w_out = lax.map(expert_work, (to_experts(normed), to_experts(delta), w_in, w_out))
    token_out = to_tokens(outputs)
    token_grad = to_tokens(grads)
    grad_gate = jnp.where(kept_mask, lax.optimization_barrier(jnp.sum(grad_float * token_out.astype(jnp.float32), axis=-1)), 0.0).astype(jnp.bfloat16)
    branch = jnp.where(kept_mask[..., None], norm_backward(token_grad, scaled, spread, gain), 0.0)
    grad_tokens = (grad_float + branch).astype(jnp.bfloat16)
    return (grad_tokens.reshape(TOKENS, D), grad_gate.reshape(TOKENS), grad_w_in, grad_w_out)
```

```python
import functools

import jax
import jax.numpy as jnp
from jax import lax
from jax.experimental import pallas as pl
from jax.experimental.pallas import tpu as pltpu
from jax.sharding import PartitionSpec as P

MESH = pl.DeviceIdType.MESH
F32 = jnp.float32
BF16 = jnp.bfloat16
EPS = 1e-05
CAP = 24
TOK = 576
D = 512
FF = 1024
ROWS = 32 * CAP
SLICE = FF // 16


def coordinates():
    space, group = lax.axis_index("space"), lax.axis_index("dp")
    return space // 8, group // 4, ((space // 2) % 4) * 4 + group % 4, space % 2


def device(x, y, z, c):
    return {"space": (x * 4 + z // 4) * 2 + c, "dp": y * 4 + z % 4}


def nt(left, right):
    return lax.dot_general(left, right, (((1,), (1,)), ((), ())), preferred_element_type=F32)


def tn(left, right):
    return lax.dot_general(left, right, (((0,), (0,)), ((), ())), preferred_element_type=F32)


def nn(left, right):
    return lax.dot_general(left, right, (((1,), (0,)), ((), ())), preferred_element_type=F32)


def iota(shape, dim):
    return lax.broadcasted_iota(jnp.int32, shape, dim).astype(F32)


def kernel(
    tok, gain, win, wout, ids, gate, gout,
    gtok, ggate, gwin, gwout,
    scaled_ref, col_ref, pair_ref, row_ref, sbuf, rbuf, xbuf, dbuf,
    wsend, wbuf, act_ref, gp_ref, dx_ref, gd_ref, gbuf, rl, rr,
    rt, bk, fsend, fout, pw, pout,
    disp_s, disp_r, ret_s, ret_r, pre_s, pre_r, ag_s, ag_r, rl_s, rl_r, rr_s, rr_r, fin_s, fin_r, fo_s, fo_r,
):
    x, y, z, c = coordinates()
    zh, zl = z // 4, z % 4
    me = x * 8 + y * 2 + c
    group = y * 4 + zl
    home = y == zh
    right, left = device(x, y, (z + 1) % 16, c), device(x, y, (z + 15) % 16, c)
    swap = device(x, zh, y * 4 + zl, c)

    barrier = pltpu.get_barrier_semaphore()

    def greet(to):
        pl.semaphore_signal(barrier, inc=1, device_id=to, device_id_type=MESH)

    def peer(j):
        px, py, pc = (x + j // 8) % 4, (y + (j // 2) % 4) % 4, (c + j) % 2
        return device(px, py, z, pc), px * 8 + py * 2 + pc

    greet(right)
    greet(left)

    @pl.loop(1, 32)
    def _(j):
        greet(peer(j)[0])

    @pl.loop(0, 16)
    def _(j):
        @pl.when(jnp.logical_not(home & (j == z)))
        def _():
            greet(device(x, zh, j, c))

    @pl.when(jnp.logical_not(home))
    def _():
        greet(swap)

    expert = ids[...].astype(F32)
    onehot = (expert == iota((TOK, 128), 1)).astype(F32)
    earlier = (iota((TOK, TOK), 0) > iota((TOK, TOK), 1)).astype(F32).astype(BF16)
    before = nn(earlier, onehot.astype(BF16))
    clipped = jnp.minimum(before, float(CAP)) * onehot
    rank = jnp.sum(clipped, axis=1, keepdims=True)
    kept = rank < float(CAP)
    expert_row = nt(iota((8, 128), 1).astype(BF16), onehot.astype(BF16))
    rank_row = nt(jnp.ones((8, 128), BF16), clipped.astype(BF16))
    row_ref[...] = jnp.where(rank_row < float(CAP), expert_row * float(CAP) + rank_row, -1.0)
    same = (iota((TOK, TOK), 0) == iota((TOK, TOK), 1)).astype(F32).astype(BF16)
    gate_col = nt(same, jnp.broadcast_to(gate[...], (8, TOK)))[:, 0:1]
    col_ref[...] = jnp.where(
        iota((TOK, 128), 1) == 0.0,
        expert,
        jnp.where(iota((TOK, 128), 1) == 1.0, rank, gate_col),
    )

    @pl.loop(0, 4)
    def _(i):
        at = pl.ds(pl.multiple_of(i * 144, 16), 144)
        values = tok[at, :].astype(F32)
        center = values - jnp.mean(values, axis=1, keepdims=True)
        spread = lax.rsqrt(jnp.mean(center * center, axis=1, keepdims=True) + EPS)
        scaled = center * spread
        scaled_ref[at, 0:D] = scaled
        scaled_ref[at, D : D + 128] = jnp.broadcast_to(spread, (144, 128))
        pair_ref[at, 0:D] = (scaled * gain[...]).astype(BF16)
        pair_ref[at, D : 2 * D] = (col_ref[at, 2:3] * gout[at, :].astype(F32)).astype(BF16)

    half = (group % 2).astype(F32)
    block = win[:, pl.ds(pl.multiple_of((group // 2) * 128, 128), 128)].astype(F32).T
    chosen = block[0:SLICE] * (1.0 - half) + block[SLICE : 2 * SLICE] * half
    wsend[0:SLICE, :] = chosen.astype(BF16)
    wsend[SLICE : 2 * SLICE, :] = wout[pl.ds(pl.multiple_of(group * SLICE, SLICE), SLICE), :]

    pl.semaphore_wait(barrier, jnp.where(home, 48, 50))

    pre = pltpu.make_async_remote_copy(
        src_ref=wsend, dst_ref=wbuf.at[group], send_sem=pre_s, recv_sem=pre_r,
        device_id=swap, device_id_type=MESH,
    )

    @pl.when(jnp.logical_not(home))
    def _():
        pre.start()

    @pl.when(home)
    def _():
        wbuf[group] = wsend[...]

    def dispatch(j):
        to, index = peer(j)
        return pltpu.make_async_remote_copy(
            src_ref=sbuf.at[index], dst_ref=rbuf.at[me], send_sem=disp_s.at[j], recv_sem=disp_r.at[j],
            device_id=to, device_id_type=MESH,
        )

    @pl.loop(0, 4)
    def _(i):
        dx = (i + 1) % 4
        first = ((x + dx) % 4) * 8
        slots = iota((8 * CAP, TOK), 0) + (first * CAP).astype(F32)
        chosen = (slots == row_ref[0:1, :]).astype(F32).astype(BF16)
        placed = nn(chosen, pair_ref[...])
        for e in range(8):
            rows = placed[e * CAP : (e + 1) * CAP]
            sbuf[first + e] = jnp.concatenate([rows[:, 0:D], rows[:, D : 2 * D]], axis=0).astype(BF16)

        @pl.loop(jnp.where(dx == 0, 1, 0), 8)
        def _(j):
            dispatch(dx * 8 + j).start()

    rbuf[me] = sbuf[me]

    def gather(a, h, way):
        return pltpu.make_async_remote_copy(
            src_ref=wbuf.at[a, pl.ds(h * SLICE, SLICE)], dst_ref=wbuf.at[a, pl.ds(h * SLICE, SLICE)],
            send_sem=ag_s.at[way, a, h], recv_sem=ag_r.at[a, h],
            device_id=(right, left)[way], device_id_type=MESH,
        )

    @pl.when(jnp.logical_not(home))
    def _():
        pltpu.make_async_remote_copy(
            src_ref=wsend, dst_ref=wbuf.at[z], send_sem=pre_s, recv_sem=pre_r,
            device_id=swap, device_id_type=MESH,
        ).wait_recv()

    for h in range(2):
        gather(z, h, 0).start()
        gather(z, h, 1).start()

    def hop(k):
        a, b = (z + 16 - k) % 16, (z + k) % 16
        for h in range(2):
            gather(a, h, 0).wait_recv()

            @pl.when(k < 8)
            def _(h=h):
                gather(a, h, 0).start()
                gather(b, h, 1).wait_recv()

                @pl.when(k < 7)
                def _():
                    gather(b, h, 1).start()

    @pl.loop(1, 5)
    def _(k):
        hop(k)

    @pl.loop(0, 16)
    def _(m):
        dx, dy = m // 4, m % 4
        for dc in range(2):
            @pl.when(m * 2 + dc > 0)
            def _(dc=dc):
                dispatch(m * 2 + dc).wait_recv()

        sx, sy = (x + 4 - dx) % 4, (y + 4 - dy) % 4
        n = sx * 4 + sy
        one, two = rbuf[n * 2].astype(F32), rbuf[n * 2 + 1].astype(F32)
        xbuf[n] = jnp.concatenate([one[0:CAP], two[0:CAP]], axis=0).astype(BF16)
        dbuf[n] = jnp.concatenate([one[CAP : 2 * CAP], two[CAP : 2 * CAP]], axis=0).astype(BF16)

    def reduce_left(s, h, src):
        return pltpu.make_async_remote_copy(
            src_ref=src.at[pl.ds(h * SLICE, SLICE)], dst_ref=rl.at[s, pl.ds(h * SLICE, SLICE)],
            send_sem=rl_s.at[s, h], recv_sem=rl_r.at[s, h], device_id=left, device_id_type=MESH,
        )

    def reduce_right(s, h, src):
        return pltpu.make_async_remote_copy(
            src_ref=src.at[pl.ds(h * SLICE, SLICE)], dst_ref=rr.at[s, pl.ds(h * SLICE, SLICE)],
            send_sem=rr_s.at[s, h], recv_sem=rr_r.at[s, h], device_id=right, device_id_type=MESH,
        )

    def reduce_step(s):
        for h in range(2):
            at = pl.ds(h * SLICE, SLICE)

            @pl.when(s == 0)
            def _(h=h):
                reduce_left(0, h, gbuf.at[0]).start()
                reduce_right(0, h, gbuf.at[1]).start()

            @pl.when(s > 0)
            def _(h=h, at=at):
                reduce_left(s - 1, h, gbuf.at[0]).wait_recv()
                rl[s - 1, at] = (rl[s - 1, at].astype(F32) + gbuf[2 * s, at].astype(F32)).astype(BF16)
                reduce_left(s, h, rl.at[s - 1]).start()

            @pl.when((s > 0) & (s < 7))
            def _(h=h, at=at):
                reduce_right(s - 1, h, gbuf.at[0]).wait_recv()
                rr[s - 1, at] = (rr[s - 1, at].astype(F32) + gbuf[2 * s + 1, at].astype(F32)).astype(BF16)
                reduce_right(s, h, rr.at[s - 1]).start()

    @pl.loop(0, 4)
    def _(g):
        hop(g + 5)
        held = [(z + 2 * g) % 16, (z + 15 - 2 * g) % 16, (z + 2 * g + 1) % 16, (z + 14 - 2 * g) % 16]
        w_in = jnp.concatenate([wbuf[a, 0:SLICE] for a in held], axis=0)
        w_out = jnp.concatenate([wbuf[a, SLICE : 2 * SLICE] for a in held], axis=0)

        @pl.loop(0, 4)
        def _(i):
            four = pl.ds(i * 4, 4)
            at = pl.ds(pl.multiple_of(i * 192, 16), 192)
            pre_act = nt(xbuf[four].reshape(192, D), w_in)
            grad_act = nt(dbuf[four].reshape(192, D), w_out)
            square = pre_act * pre_act
            curve = jnp.tanh(0.7978845608028654 * pre_act * (1.0 + 0.044715 * square))
            half_up = 0.5 * (1.0 + curve)
            activity = (pre_act * half_up).astype(BF16)
            slope = half_up + 0.5 * pre_act * (1.0 - curve * curve) * (
                0.7978845608028654 * (1.0 + 3 * 0.044715 * square)
            )
            grad_pre = (grad_act * slope).astype(BF16)
            act_ref[at, :] = activity
            gp_ref[at, :] = grad_pre
            dot = jnp.sum(activity.astype(F32) * grad_act, axis=1, keepdims=True)
            back = nn(grad_pre, w_in)

            @pl.when(g == 0)
            def _():
                gd_ref[at, :] = jnp.broadcast_to(dot, (192, 128))
                dx_ref[at, :] = back

            @pl.when(g > 0)
            def _():
                gd_ref[at, :] += jnp.broadcast_to(dot, (192, 128))
                dx_ref[at, :] += back

        part_in = tn(gp_ref[...], xbuf[...].reshape(ROWS, D)).astype(BF16)
        part_out = tn(act_ref[...], dbuf[...].reshape(ROWS, D)).astype(BF16)
        for j in range(4):
            gbuf[4 * g + j, 0:SLICE] = part_in[j * SLICE : (j + 1) * SLICE]
            gbuf[4 * g + j, SLICE : 2 * SLICE] = part_out[j * SLICE : (j + 1) * SLICE]
        reduce_step(2 * g)

        @pl.when(g < 3)
        def _():
            reduce_step(2 * g + 1)

    place = iota((ROWS, 128), 0) - jnp.floor(iota((ROWS, 128), 0) * (1.0 / CAP) + 0.5 / CAP) * CAP
    lane = iota((ROWS, 128), 1)
    total = gd_ref[...]
    high = total.astype(BF16).astype(F32)
    spread_out = jnp.where(lane == place, high, jnp.where(lane == place + 32.0, total - high, 0.0)).astype(BF16)
    owner = iota((32, ROWS), 1) - iota((32, ROWS), 0) * CAP
    pick = ((owner >= 0.0) & (owner < float(CAP))).astype(F32).astype(BF16)
    gd_ref[0:32, :] = nn(pick, spread_out)

    def give_back(j):
        to, index = peer(j)
        return pltpu.make_async_remote_copy(
            src_ref=rt.at[index], dst_ref=bk.at[me], send_sem=ret_s.at[j], recv_sem=ret_r.at[j],
            device_id=to, device_id_type=MESH,
        )

    @pl.loop(0, 32)
    def _(j):
        index = peer(j)[1]
        rows = dx_ref[pl.ds(pl.multiple_of(index * CAP, 8), CAP), :]
        extra = jnp.broadcast_to(gd_ref[pl.ds(index, 1), :], (8, 128))
        extra = jnp.concatenate([extra, jnp.zeros((8, D - 128), F32)], axis=1)
        rt[index] = jnp.concatenate([rows, extra], axis=0).astype(BF16)

        @pl.when(j > 0)
        def _():
            give_back(j).start()

    bk[me] = rt[me]

    reduce_step(jnp.int32(7))

    for h in range(2):
        reduce_left(7, h, gbuf.at[0]).wait_recv()
        reduce_right(6, h, gbuf.at[0]).wait_recv()
    summed = rl[7].astype(F32) + rr[6].astype(F32) + gbuf[15].astype(F32)
    fout[...] = summed[SLICE : 2 * SLICE].astype(BF16)
    turned = summed[0:SLICE].T.reshape(16, 32, SLICE)
    fsend[...] = jnp.concatenate([turned[:, 0:16], turned[:, 16:32]], axis=2).astype(BF16)

    def keep_in(j):
        return pltpu.make_async_remote_copy(
            src_ref=fsend.at[j], dst_ref=pw.at[z], send_sem=fin_s.at[j], recv_sem=fin_r.at[z],
            device_id=device(x, j // 4, y * 4 + j % 4, c), device_id_type=MESH,
        )

    def came_in(j):
        return pltpu.make_async_remote_copy(
            src_ref=fsend.at[j], dst_ref=pw.at[j], send_sem=fin_s.at[j], recv_sem=fin_r.at[j],
            device_id=right, device_id_type=MESH,
        )

    kept_slice = (z + 8) % 16
    keep_out = pltpu.make_async_remote_copy(
        src_ref=fout, dst_ref=pout, send_sem=fo_s, recv_sem=fo_r,
        device_id=device(x, kept_slice // 4, y * 4 + kept_slice % 4, c), device_id_type=MESH,
    )
    keep_out.start()

    @pl.loop(0, 16)
    def _(j):
        here = home & (j == group)

        @pl.when(jnp.logical_not(here))
        def _():
            keep_in(j).start()

        @pl.when(here)
        def _():
            pw[z] = fsend[j]

    @pl.loop(1, 32)
    def _(j):
        give_back(j).wait_recv()

    @pl.loop(0, 3)
    def _(i):
        at = pl.ds(pl.multiple_of(i * 192, 16), 192)
        expert, rank = col_ref[at, 0:1], col_ref[at, 1:2]
        kept = rank < float(CAP)
        slot = iota((192, 1024), 1)
        returned = bk[...].reshape(1024, D)
        chosen = (slot == jnp.where(kept, expert * 32.0 + rank, -1.0)).astype(F32).astype(BF16)
        token_grad = nn(chosen, returned)
        line = (slot == expert * 32.0 + float(CAP)).astype(F32).astype(BF16)
        products = nn(line, returned[:, 0:128])
        lane = iota((192, 128), 1)
        product = jnp.sum(
            jnp.where((lane == rank) | (lane == rank + 32.0), products, 0.0), axis=1, keepdims=True
        )
        scaled, spread = scaled_ref[at, 0:D], scaled_ref[at, D : D + 1]
        u = token_grad * gain[...]
        mean = jnp.mean(u, axis=1, keepdims=True)
        cross = jnp.mean(u * scaled, axis=1, keepdims=True)
        branch = jnp.where(kept, spread * (u - mean - scaled * cross), 0.0)
        gtok[at, :] = (gout[at, :].astype(F32) + branch).astype(BF16)
        answer = jnp.where(kept, product / col_ref[at, 2:3], 0.0)
        top = answer.astype(BF16).astype(F32)
        col_ref[at, :] = jnp.where(lane == 0.0, top, jnp.where(lane == 1.0, answer - top, 0.0))

    ggate[...] = nt(jnp.ones((8, 128), BF16), col_ref[...].astype(BF16))[0:1, :].astype(BF16)

    for j in range(8):
        wide = []
        for f in (2 * j, 2 * j + 1):
            at = (f + 8) % 16

            @pl.when(jnp.logical_not(home & (z == at)))
            def _(at=at):
                came_in(at).wait_recv()

            wide.append(pw[at].astype(F32))
        upper = jnp.concatenate([wide[0][:, 0:SLICE], wide[1][:, 0:SLICE]], axis=1)
        lower = jnp.concatenate([wide[0][:, SLICE : 2 * SLICE], wide[1][:, SLICE : 2 * SLICE]], axis=1)
        gwin[0:16, j * 128 : (j + 1) * 128] = upper
        gwin[16:32, j * 128 : (j + 1) * 128] = lower
    keep_out.wait_recv()
    gwout[...] = pout[...].astype(F32)

    @pl.when(jnp.logical_not(home))
    def _():
        pre.wait_send()

    @pl.loop(1, 32)
    def _(j):
        dispatch(j).wait_send()
        give_back(j).wait_send()

    @pl.loop(0, 8)
    def _(k):
        for h in range(2):
            gather((z + 16 - k) % 16, h, 0).wait_send()
            reduce_left(k, h, gbuf.at[0]).wait_send()

            @pl.when(k < 7)
            def _(h=h):
                gather((z + k) % 16, h, 1).wait_send()
                reduce_right(k, h, gbuf.at[0]).wait_send()

    @pl.loop(0, 16)
    def _(j):
        @pl.when(jnp.logical_not(home & (j == group)))
        def _():
            keep_in(j).wait_send()

    keep_out.wait_send()


def body(tokens, gain, w_in, w_out, expert_ids, gate, grad_out):
    vmem = pl.BlockSpec(memory_space=pltpu.VMEM)
    dma = pltpu.SemaphoreType.DMA
    scratch = [
        ((TOK, D + 128), F32), ((TOK, 128), F32), ((TOK, 2 * D), BF16), ((8, TOK), F32),
        ((32, 2 * CAP, D), BF16), ((32, 2 * CAP, D), BF16), ((16, 2 * CAP, D), BF16), ((16, 2 * CAP, D), BF16),
        ((2 * SLICE, D), BF16), ((16, 2 * SLICE, D), BF16), ((ROWS, 4 * SLICE), BF16), ((ROWS, 4 * SLICE), BF16),
        ((ROWS, D), F32), ((ROWS, 128), F32), ((16, 2 * SLICE, D), BF16),
        ((8, 2 * SLICE, D), BF16), ((7, 2 * SLICE, D), BF16),
        ((32, 32, D), BF16), ((32, 32, D), BF16), ((16, 16, 128), BF16), ((SLICE, D), BF16),
        ((16, 16, 128), BF16), ((SLICE, D), BF16),
    ]
    semaphores = [
        dma((32,)), dma((32,)), dma((32,)), dma((32,)), dma, dma, dma((2, 16, 2)), dma((16, 2)),
        dma((8, 2)), dma((8, 2)), dma((7, 2)), dma((7, 2)), dma((16,)), dma((16,)), dma, dma,
    ]
    out = pl.pallas_call(
        kernel,
        out_shape=(
            jax.ShapeDtypeStruct((TOK, D), BF16),
            jax.ShapeDtypeStruct((1, TOK), BF16),
            jax.ShapeDtypeStruct((D // 16, FF), F32),
            jax.ShapeDtypeStruct((SLICE, D), F32),
        ),
        in_specs=[vmem] * 7,
        out_specs=(vmem,) * 4,
        scratch_shapes=[pltpu.VMEM(shape, kind) for shape, kind in scratch] + semaphores,
        compiler_params=pltpu.CompilerParams(
            collective_id=0, has_side_effects=True, vmem_limit_bytes=56 * 1024 * 1024
        ),
        cost_estimate=pl.CostEstimate(flops=5 * 10**9, bytes_accessed=6 * 10**6, transcendentals=10**6),
    )(tokens, gain.reshape(1, D), w_in[0], w_out[0], expert_ids, gate.reshape(1, TOK), grad_out)
    return out[0], out[1].reshape(TOK), out[2][None], out[3][None]


def solution(mesh):
    placed = (
        P(("space", "dp"), None),
        P(),
        P("space", None, None),
        P("space", None, None),
        P(("space", "dp"), None),
        P(("space", "dp")),
        P(("space", "dp"), None),
    )
    return jax.shard_map(
        body,
        mesh=mesh,
        in_specs=placed,
        out_specs=(
            P(("space", "dp"), None),
            P(("space", "dp")),
            P("space", "dp", None),
            P("space", "dp", None),
        ),
        check_vma=False,
    )
```

```python
import functools

import jax
import jax.numpy as jnp
from jax import lax
from jax.experimental import pallas as pl
from jax.experimental.pallas import tpu as pltpu
from jax.sharding import PartitionSpec as P

MESH = pl.DeviceIdType.MESH
F32 = jnp.float32
BF16 = jnp.bfloat16
EPS = 1e-05
CAP = 24
TOK = 576
D = 512
FF = 1024
ROWS = 32 * CAP
SLICE = FF // 16


def coordinates():
    space, group = lax.axis_index("space"), lax.axis_index("dp")
    return space // 8, group // 4, ((space // 2) % 4) * 4 + group % 4, space % 2


def device(x, y, z, c):
    return {"space": (x * 4 + z // 4) * 2 + c, "dp": y * 4 + z % 4}


def nt(left, right):
    return lax.dot_general(left, right, (((1,), (1,)), ((), ())), preferred_element_type=F32)


def tn(left, right):
    return lax.dot_general(left, right, (((0,), (0,)), ((), ())), preferred_element_type=F32)


def nn(left, right):
    return lax.dot_general(left, right, (((1,), (0,)), ((), ())), preferred_element_type=F32)


def iota(shape, dim):
    return lax.broadcasted_iota(jnp.int32, shape, dim).astype(F32)


def kernel(
    tok_hbm, gain, win, wout, ids, gate, gout_hbm,
    gtok, ggate, gwin, gwout,
    tok, gout, blocks, wide, scaled_ref, col_ref, pair_ref, row_ref, sbuf, rbuf, xbuf, dbuf,
    wsend, wbuf, act_ref, gp_ref, dx_ref, gd_ref, gbuf, rl, rr,
    rt, bk, fsend, fout, mid_in, mid_out, pw, pout, gtok_v, gwin_v, gwout_v,
    tok_c, gout_c, wide_c, disp_s, disp_r, ret_s, ret_r, pre_s, pre_r, ag_s, ag_r, rl_s, rl_r, rr_s, rr_r, fin_s, fin_r, fo_s, fo_r,
    mi_s, mi_r, mo_s, mo_r,
):
    x, y, z, c = coordinates()
    zh, zl = z // 4, z % 4
    me = x * 8 + y * 2 + c
    group = y * 4 + zl
    home = y == zh
    right, left = device(x, y, (z + 1) % 16, c), device(x, y, (z + 15) % 16, c)
    away = jnp.logical_not(home)
    offset = (z + 16 - 4 * y) % 16

    into_tok = pltpu.make_async_copy(tok_hbm, tok, tok_c)
    into_gout = pltpu.make_async_copy(gout_hbm, gout, gout_c)
    into_tok.start()
    into_gout.start()

    def flip(v):
        return v + 1 - 2 * (v % 2)

    def slice_of(a, k):
        return ((a // 4 + 6 - k) % 4) * 4 + flip(a % 4)

    def plane_of(f, k):
        return ((f // 4 + 2 + k) % 4) * 4 + flip(f % 4)

    def block_in(n, a):
        return pltpu.make_async_copy(
            win.at[:, pl.ds(pl.multiple_of((a // 2) * 128, 128), 128)], blocks.at[n], wide_c.at[n]
        )

    def rows_in(n, a):
        return pltpu.make_async_copy(
            wout.at[pl.ds(pl.multiple_of(a * SLICE, SLICE), SLICE)], wsend.at[n, 1], wide_c.at[2 + n]
        )

    outer = (zl == 0) | (zl == 3)
    column = jnp.where(zl == 3, y + 4 - zh, y + 6 - zh) % 4
    reach = (jnp.where(column == 0, 4, column), jnp.where(column == 0, 8, column + 4))
    aims = [jnp.where(zl == 3, z + r, z + 16 - r) % 16 for r in reach]
    sends = [outer & (r <= 6) for r in reach]

    for n in range(2):
        @pl.when(sends[n])
        def _(n=n):
            block_in(n, slice_of(aims[n], zh)).start()
            rows_in(n, slice_of(aims[n], zh)).start()

    whole_in = pltpu.make_async_copy(win, wide, wide_c.at[4])

    def home_rows(f):
        return pltpu.make_async_copy(
            wout.at[pl.ds(pl.multiple_of(f * SLICE, SLICE), SLICE)], wbuf.at[plane_of(f, y), 1], wide_c.at[5 + f]
        )

    @pl.when(home)
    def _():
        whole_in.start()

        @pl.loop(0, 16)
        def _(f):
            home_rows(f).start()

    barrier = pltpu.get_barrier_semaphore()

    def greet(to):
        pl.semaphore_signal(barrier, inc=1, device_id=to, device_id_type=MESH)

    def peer(j):
        px, py, pc = (x + j // 8) % 4, (y + (j // 2) % 4) % 4, (c + j) % 2
        return device(px, py, z, pc), px * 8 + py * 2 + pc

    @pl.loop(1, 32)
    def _(j):
        greet(peer(j)[0])

    @pl.loop(1, 16)
    def _(j):
        greet(device(x, y, (z + j) % 16, c))

    near = jnp.where(offset < 10, offset - 3, 16 - offset)
    giver = jnp.where(
        offset < 10,
        device(x, (y + near) % 4, (4 * y + 3) % 16, c)["space"],
        device(x, (y + near + 2) % 4, 4 * y, c)["space"],
    )
    giver_group = jnp.where(offset < 10, ((y + near) % 4) * 4 + 3, ((y + near + 2) % 4) * 4)
    giver = {"space": giver, "dp": giver_group}

    @pl.when(away)
    def _():
        greet(giver)

    def gather(a, h, way):
        return pltpu.make_async_remote_copy(
            src_ref=wbuf.at[a, h], dst_ref=wbuf.at[a, h],
            send_sem=ag_s.at[way, a, h], recv_sem=ag_r.at[a, h],
            device_id=(right, left)[way], device_id_type=MESH,
        )

    def pre(n):
        return pltpu.make_async_remote_copy(
            src_ref=wsend.at[n], dst_ref=wbuf.at[aims[n]], send_sem=pre_s.at[n], recv_sem=pre_r,
            device_id=device(x, zh, aims[n], c), device_id_type=MESH,
        )

    for n in range(2):
        @pl.when(sends[n])
        def _(n=n):
            block_in(n, slice_of(aims[n], zh)).wait()
            rows_in(n, slice_of(aims[n], zh)).wait()
            half = (slice_of(aims[n], zh) % 2).astype(F32)
            turned = blocks[n].astype(F32).T
            wsend[n, 0] = (turned[0:SLICE] * (1.0 - half) + turned[SLICE : 2 * SLICE] * half).astype(BF16)

    @pl.when(home)
    def _():
        whole_in.wait()
        for j in range(8):
            turned = wide[:, j * 128 : (j + 1) * 128].astype(F32).T.astype(BF16)
            wbuf[plane_of(2 * j, y), 0] = turned[0:SLICE]
            wbuf[plane_of(2 * j + 1, y), 0] = turned[SLICE : 2 * SLICE]

        @pl.loop(0, 16)
        def _(f):
            home_rows(f).wait()

    aimed = jnp.where(sends[0], 1, 0) + jnp.where(sends[1], 1, 0)
    pl.semaphore_wait(barrier, 46 + aimed)

    for n in range(2):
        @pl.when(sends[n])
        def _(n=n):
            pre(n).start()

    @pl.when(home)
    def _():
        @pl.when(zl == 3)
        def _():
            @pl.loop(0, 8)
            def _(k):
                for h in range(2):
                    gather((z + 16 - k) % 16, h, 0).start()

        @pl.when(zl == 0)
        def _():
            @pl.loop(0, 7)
            def _(k):
                for h in range(2):
                    gather((z + k) % 16, h, 1).start()

    same = (iota((TOK, TOK), 0) == iota((TOK, TOK), 1)).astype(F32).astype(BF16)
    lines = jnp.where(iota((8, TOK), 0) == 0.0, ids[...].astype(F32), gate[...].astype(F32).reshape(1, TOK))
    columns = nt(same, lines.astype(BF16))
    expert, gate_col = columns[:, 0:1], columns[:, 1:2]
    onehot = (expert == iota((TOK, 128), 1)).astype(F32)
    earlier = (iota((TOK, TOK), 0) > iota((TOK, TOK), 1)).astype(F32).astype(BF16)
    before = nn(earlier, onehot.astype(BF16))
    clipped = jnp.minimum(before, float(CAP)) * onehot
    rank = jnp.sum(clipped, axis=1, keepdims=True)
    kept = rank < float(CAP)
    expert_row = ids[...].astype(F32)
    rank_row = nt(jnp.ones((8, 128), BF16), clipped.astype(BF16))
    row_ref[...] = jnp.where(rank_row < float(CAP), expert_row * float(CAP) + rank_row, -1.0)
    col_ref[...] = jnp.where(
        iota((TOK, 128), 1) == 0.0,
        expert,
        jnp.where(iota((TOK, 128), 1) == 1.0, rank, gate_col),
    )

    into_tok.wait()
    into_gout.wait()

    @pl.loop(0, 4)
    def _(i):
        at = pl.ds(pl.multiple_of(i * 144, 16), 144)
        values = tok[at, :].astype(F32)
        center = values - jnp.mean(values, axis=1, keepdims=True)
        spread = lax.rsqrt(jnp.mean(center * center, axis=1, keepdims=True) + EPS)
        scaled = center * spread
        scaled_ref[at, 0:D] = scaled
        scaled_ref[at, D : D + 128] = jnp.broadcast_to(spread, (144, 128))
        pair_ref[at, 0:D] = (scaled * gain[...]).astype(BF16)
        pair_ref[at, D : 2 * D] = (col_ref[at, 2:3] * gout[at, :].astype(F32)).astype(BF16)

    last_right, last_left = offset == 15, offset == 4

    def own_slice():
        pltpu.make_async_remote_copy(
            src_ref=wsend.at[0], dst_ref=wbuf.at[z], send_sem=pre_s.at[0], recv_sem=pre_r,
            device_id=right, device_id_type=MESH,
        ).wait_recv()
        for h in range(2):
            @pl.when(jnp.logical_not(last_right))
            def _(h=h):
                gather(z, h, 0).start()

            @pl.when(jnp.logical_not(last_left))
            def _(h=h):
                gather(z, h, 1).start()

    def hop(k):
        a, b = (z + 16 - k) % 16, (z + k) % 16

        @pl.when(away)
        def _():
            for h in range(2):
                gather(a, h, 0).wait_recv()

                @pl.when((k < 8) & jnp.logical_not(last_right))
                def _(h=h):
                    gather(a, h, 0).start()

                @pl.when(k < 8)
                def _(h=h):
                    gather(b, h, 1).wait_recv()

                @pl.when((k < 7) & jnp.logical_not(last_left))
                def _(h=h):
                    gather(b, h, 1).start()

    def dispatch(j):
        to, index = peer(j)
        return pltpu.make_async_remote_copy(
            src_ref=sbuf.at[index], dst_ref=rbuf.at[me], send_sem=disp_s.at[j], recv_sem=disp_r.at[j],
            device_id=to, device_id_type=MESH,
        )

    @pl.loop(0, 4)
    def _(i):
        @pl.when((i == 1) & away)
        def _():
            own_slice()

        @pl.when(i == 3)
        def _():
            hop(1)

        dx = (i + 1) % 4
        first = ((x + dx) % 4) * 8
        slots = iota((8 * CAP, TOK), 0) + (first * CAP).astype(F32)
        chosen = (slots == row_ref[0:1, :]).astype(F32).astype(BF16)
        placed = nn(chosen, pair_ref[...])
        for e in range(8):
            rows = placed[e * CAP : (e + 1) * CAP]
            sbuf[first + e] = jnp.concatenate([rows[:, 0:D], rows[:, D : 2 * D]], axis=0).astype(BF16)

        @pl.loop(jnp.where(dx == 0, 1, 0), 8)
        def _(j):
            dispatch(dx * 8 + j).start()

    rbuf[me] = sbuf[me]

    hop(2)
    hop(3)
    hop(4)

    @pl.loop(0, 16)
    def _(m):
        dx, dy = m // 4, m % 4
        for dc in range(2):
            @pl.when(m * 2 + dc > 0)
            def _(dc=dc):
                dispatch(m * 2 + dc).wait_recv()

        sx, sy = (x + 4 - dx) % 4, (y + 4 - dy) % 4
        n = sx * 4 + sy
        one, two = rbuf[n * 2].astype(F32), rbuf[n * 2 + 1].astype(F32)
        xbuf[n] = jnp.concatenate([one[0:CAP], two[0:CAP]], axis=0).astype(BF16)
        dbuf[n] = jnp.concatenate([one[CAP : 2 * CAP], two[CAP : 2 * CAP]], axis=0).astype(BF16)

    def reduce_left(s, h, src):
        return pltpu.make_async_remote_copy(
            src_ref=src.at[pl.ds(h * SLICE, SLICE)], dst_ref=rl.at[s, pl.ds(h * SLICE, SLICE)],
            send_sem=rl_s.at[s, h], recv_sem=rl_r.at[s, h], device_id=left, device_id_type=MESH,
        )

    def reduce_right(s, h, src):
        return pltpu.make_async_remote_copy(
            src_ref=src.at[pl.ds(h * SLICE, SLICE)], dst_ref=rr.at[s, pl.ds(h * SLICE, SLICE)],
            send_sem=rr_s.at[s, h], recv_sem=rr_r.at[s, h], device_id=right, device_id_type=MESH,
        )

    def reduce_step(s):
        for h in range(2):
            at = pl.ds(h * SLICE, SLICE)

            @pl.when(s == 0)
            def _(h=h):
                reduce_left(0, h, gbuf.at[0]).start()
                reduce_right(0, h, gbuf.at[1]).start()

            @pl.when(s > 0)
            def _(h=h, at=at):
                reduce_left(s - 1, h, gbuf.at[0]).wait_recv()
                rl[s - 1, at] = (rl[s - 1, at].astype(F32) + gbuf[2 * s, at].astype(F32)).astype(BF16)
                reduce_left(s, h, rl.at[s - 1]).start()

            @pl.when((s > 0) & (s < 7))
            def _(h=h, at=at):
                reduce_right(s - 1, h, gbuf.at[0]).wait_recv()
                rr[s - 1, at] = (rr[s - 1, at].astype(F32) + gbuf[2 * s + 1, at].astype(F32)).astype(BF16)
                reduce_right(s, h, rr.at[s - 1]).start()

    @pl.loop(0, 4)
    def _(g):
        hop(g + 5)
        held = [(z + 2 * g) % 16, (z + 15 - 2 * g) % 16, (z + 2 * g + 1) % 16, (z + 14 - 2 * g) % 16]
        w_in = jnp.concatenate([wbuf[a, 0] for a in held], axis=0)
        w_out = jnp.concatenate([wbuf[a, 1] for a in held], axis=0)

        @pl.loop(0, 4)
        def _(i):
            four = pl.ds(i * 4, 4)
            at = pl.ds(pl.multiple_of(i * 192, 16), 192)
            pre_act = nt(xbuf[four].reshape(192, D), w_in)
            grad_act = nt(dbuf[four].reshape(192, D), w_out)
            square = pre_act * pre_act
            curve = jnp.tanh(0.7978845608028654 * pre_act * (1.0 + 0.044715 * square))
            half_up = 0.5 * (1.0 + curve)
            activity = (pre_act * half_up).astype(BF16)
            slope = half_up + 0.5 * pre_act * (1.0 - curve * curve) * (
                0.7978845608028654 * (1.0 + 3 * 0.044715 * square)
            )
            grad_pre = (grad_act * slope).astype(BF16)
            act_ref[at, :] = activity
            gp_ref[at, :] = grad_pre
            dot = jnp.sum(activity.astype(F32) * grad_act, axis=1, keepdims=True)
            back = nn(grad_pre, w_in)

            @pl.when(g == 0)
            def _():
                gd_ref[at, :] = jnp.broadcast_to(dot, (192, 128))
                dx_ref[at, :] = back

            @pl.when(g > 0)
            def _():
                gd_ref[at, :] += jnp.broadcast_to(dot, (192, 128))
                dx_ref[at, :] += back

        part_in = tn(gp_ref[...], xbuf[...].reshape(ROWS, D)).astype(BF16)
        part_out = tn(act_ref[...], dbuf[...].reshape(ROWS, D)).astype(BF16)
        for j in range(4):
            gbuf[4 * g + j, 0:SLICE] = part_in[j * SLICE : (j + 1) * SLICE]
            gbuf[4 * g + j, SLICE : 2 * SLICE] = part_out[j * SLICE : (j + 1) * SLICE]
        reduce_step(2 * g)

        @pl.when(g < 3)
        def _():
            reduce_step(2 * g + 1)

    place = iota((ROWS, 128), 0) - jnp.floor(iota((ROWS, 128), 0) * (1.0 / CAP) + 0.5 / CAP) * CAP
    lane = iota((ROWS, 128), 1)
    total = gd_ref[...]
    high = total.astype(BF16).astype(F32)
    spread_out = jnp.where(lane == place, high, jnp.where(lane == place + 32.0, total - high, 0.0)).astype(BF16)
    owner = iota((32, ROWS), 1) - iota((32, ROWS), 0) * CAP
    pick = ((owner >= 0.0) & (owner < float(CAP))).astype(F32).astype(BF16)
    gd_ref[0:32, :] = nn(pick, spread_out)

    def give_back(j):
        to, index = peer(j)
        return pltpu.make_async_remote_copy(
            src_ref=rt.at[index], dst_ref=bk.at[me], send_sem=ret_s.at[j], recv_sem=ret_r.at[j],
            device_id=to, device_id_type=MESH,
        )

    @pl.loop(0, 32)
    def _(j):
        index = peer(j)[1]
        rows = dx_ref[pl.ds(pl.multiple_of(index * CAP, 8), CAP), :]
        extra = jnp.broadcast_to(gd_ref[pl.ds(index, 1), :], (8, 128))
        extra = jnp.concatenate([extra, jnp.zeros((8, D - 128), F32)], axis=1)
        rt[index] = jnp.concatenate([rows, extra], axis=0).astype(BF16)

        @pl.when(j > 0)
        def _():
            give_back(j).start()

    bk[me] = rt[me]

    reduce_step(jnp.int32(7))

    for h in range(2):
        reduce_left(7, h, gbuf.at[0]).wait_recv()
        reduce_right(6, h, gbuf.at[0]).wait_recv()
    summed = rl[7].astype(F32) + rr[6].astype(F32) + gbuf[15].astype(F32)
    fout[...] = summed[SLICE : 2 * SLICE].astype(BF16)
    turned = summed[0:SLICE].T.reshape(16, 32, SLICE)
    fsend[...] = jnp.concatenate([turned[:, 0:16], turned[:, 16:32]], axis=2).astype(BF16)

    owner = (zh + 4 - y) % 4

    def cross_in(p):
        return pltpu.make_async_remote_copy(
            src_ref=fsend.at[pl.ds(p * 4, 4)], dst_ref=mid_in.at[y], send_sem=mi_s.at[p], recv_sem=mi_r.at[y],
            device_id=device(x, p, z, c), device_id_type=MESH,
        )

    def crossed_in(k):
        return pltpu.make_async_remote_copy(
            src_ref=mid_in.at[k], dst_ref=mid_in.at[k], send_sem=mi_s.at[k], recv_sem=mi_r.at[k],
            device_id=right, device_id_type=MESH,
        )

    cross_out = pltpu.make_async_remote_copy(
        src_ref=fout, dst_ref=mid_out, send_sem=mo_s, recv_sem=mo_r,
        device_id=device(x, owner, z, c), device_id_type=MESH,
    )

    @pl.when(owner != y)
    def _():
        cross_out.start()

    @pl.when(owner == y)
    def _():
        mid_out[...] = fout[...]

    @pl.loop(0, 4)
    def _(p):
        @pl.when(p != y)
        def _():
            cross_in(p).start()

        @pl.when(p == y)
        def _():
            mid_in[p] = fsend[pl.ds(p * 4, 4)]

    def keep_in(j):
        return pltpu.make_async_remote_copy(
            src_ref=mid_in.at[j // 4, j % 4], dst_ref=pw.at[z], send_sem=fin_s.at[j], recv_sem=fin_r.at[z],
            device_id=device(x, y, j, c), device_id_type=MESH,
        )

    def came_in(t):
        return pltpu.make_async_remote_copy(
            src_ref=pw.at[t], dst_ref=pw.at[t], send_sem=fin_s.at[t], recv_sem=fin_r.at[t],
            device_id=right, device_id_type=MESH,
        )

    keep_out = pltpu.make_async_remote_copy(
        src_ref=mid_out, dst_ref=pout, send_sem=fo_s, recv_sem=fo_r,
        device_id=device(x, y, owner * 4 + flip(zl), c), device_id_type=MESH,
    )

    @pl.when(owner != y)
    def _():
        cross_out.wait_recv()

    keep_out.start()

    @pl.loop(0, 16)
    def _(j):
        @pl.when((j % 4 == 0) & (j // 4 != y))
        def _():
            crossed_in(j // 4).wait_recv()

        @pl.when(j != z)
        def _():
            keep_in(j).start()

        @pl.when(j == z)
        def _():
            pw[z] = mid_in[zh, zl]

    out_tok = pltpu.make_async_copy(gtok_v, gtok, tok_c)
    out_win = pltpu.make_async_copy(gwin_v, gwin, gout_c)
    out_wout = pltpu.make_async_copy(gwout_v, gwout, wide_c.at[4])

    @pl.loop(1, 32)
    def _(j):
        give_back(j).wait_recv()

    @pl.loop(0, 3)
    def _(i):
        at = pl.ds(pl.multiple_of(i * 192, 16), 192)
        expert, rank = col_ref[at, 0:1], col_ref[at, 1:2]
        kept = rank < float(CAP)
        slot = iota((192, 1024), 1)
        returned = bk[...].reshape(1024, D)
        chosen = (slot == jnp.where(kept, expert * 32.0 + rank, -1.0)).astype(F32).astype(BF16)
        token_grad = nn(chosen, returned)
        line = (slot == expert * 32.0 + float(CAP)).astype(F32).astype(BF16)
        products = nn(line, returned[:, 0:128])
        lane = iota((192, 128), 1)
        product = jnp.sum(
            jnp.where((lane == rank) | (lane == rank + 32.0), products, 0.0), axis=1, keepdims=True
        )
        scaled, spread = scaled_ref[at, 0:D], scaled_ref[at, D : D + 1]
        u = token_grad * gain[...]
        mean = jnp.mean(u, axis=1, keepdims=True)
        cross = jnp.mean(u * scaled, axis=1, keepdims=True)
        branch = jnp.where(kept, spread * (u - mean - scaled * cross), 0.0)
        gtok_v[at, :] = (gout[at, :].astype(F32) + branch).astype(BF16)
        answer = jnp.where(kept, product / col_ref[at, 2:3], 0.0)
        top = answer.astype(BF16).astype(F32)
        col_ref[at, :] = jnp.where(lane == 0.0, top, jnp.where(lane == 1.0, answer - top, 0.0))

    ggate[...] = nt(jnp.ones((8, 128), BF16), col_ref[...].astype(BF16))[0:1, :].astype(BF16)

    out_tok.start()

    @pl.loop(1, 16)
    def _(j):
        came_in((z + j) % 16).wait_recv()

    for j in range(8):
        wide_rows = [
            pw[((f // 4 + zh) % 4) * 4 + flip(f % 4)].astype(F32) for f in (2 * j, 2 * j + 1)
        ]
        upper = jnp.concatenate([wide_rows[0][:, 0:SLICE], wide_rows[1][:, 0:SLICE]], axis=1)
        lower = jnp.concatenate([wide_rows[0][:, SLICE : 2 * SLICE], wide_rows[1][:, SLICE : 2 * SLICE]], axis=1)
        gwin_v[0:16, j * 128 : (j + 1) * 128] = upper
        gwin_v[16:32, j * 128 : (j + 1) * 128] = lower
    out_win.start()
    keep_out.wait_recv()
    gwout_v[...] = pout[...].astype(F32)
    out_wout.start()

    for n in range(2):
        @pl.when(sends[n])
        def _(n=n):
            pre(n).wait_send()

    @pl.loop(1, 32)
    def _(j):
        dispatch(j).wait_send()
        give_back(j).wait_send()

    @pl.loop(0, 8)
    def _(k):
        for h in range(2):
            @pl.when(((offset > 3) & jnp.logical_not(last_right)) | (offset == 3))
            def _(h=h):
                gather((z + 16 - k) % 16, h, 0).wait_send()

            @pl.when((k < 7) & (((offset > 3) & jnp.logical_not(last_left)) | (offset == 0)))
            def _(h=h):
                gather((z + k) % 16, h, 1).wait_send()

            reduce_left(k, h, gbuf.at[0]).wait_send()

            @pl.when(k < 7)
            def _(h=h):
                reduce_right(k, h, gbuf.at[0]).wait_send()

    @pl.loop(0, 16)
    def _(j):
        @pl.when(j != z)
        def _():
            keep_in(j).wait_send()

        @pl.when((j < 4) & (j != y))
        def _():
            cross_in(j).wait_send()

    @pl.when(owner != y)
    def _():
        cross_out.wait_send()

    keep_out.wait_send()
    out_tok.wait()
    out_win.wait()
    out_wout.wait()


def finish(tok, gate, win, wout, tok_out, gate_out, win_out, wout_out):
    tok_out[...] = tok[...]
    gate_out[...] = gate[0, :]
    win_out[...] = win[...]
    wout_out[...] = wout[...]


def body(tokens, gain, w_in, w_out, expert_ids, gate, grad_out):
    vmem = pl.BlockSpec(memory_space=pltpu.VMEM)
    hbm = pl.BlockSpec(memory_space=pl.ANY)
    dma = pltpu.SemaphoreType.DMA
    scratch = [
        ((TOK, D), BF16), ((TOK, D), BF16), ((2, D, 128), BF16), ((D, FF), BF16),
        ((TOK, D + 128), F32), ((TOK, 128), F32), ((TOK, 2 * D), BF16), ((8, TOK), F32),
        ((32, 2 * CAP, D), BF16), ((32, 2 * CAP, D), BF16), ((16, 2 * CAP, D), BF16), ((16, 2 * CAP, D), BF16),
        ((2, 2, SLICE, D), BF16), ((16, 2, SLICE, D), BF16), ((ROWS, 4 * SLICE), BF16), ((ROWS, 4 * SLICE), BF16),
        ((ROWS, D), F32), ((ROWS, 128), F32), ((16, 2 * SLICE, D), BF16),
        ((8, 2 * SLICE, D), BF16), ((7, 2 * SLICE, D), BF16),
        ((32, 32, D), BF16), ((32, 32, D), BF16), ((16, 16, 128), BF16), ((SLICE, D), BF16),
        ((4, 4, 16, 128), BF16), ((SLICE, D), BF16),
        ((16, 16, 128), BF16), ((SLICE, D), BF16), ((TOK, D), BF16), ((D // 16, FF), F32), ((SLICE, D), F32),
    ]
    semaphores = [
        dma, dma, dma((21,)),
        dma((32,)), dma((32,)), dma((32,)), dma((32,)), dma((2,)), dma, dma((2, 16, 2)), dma((16, 2)),
        dma((8, 2)), dma((8, 2)), dma((7, 2)), dma((7, 2)), dma((16,)), dma((16,)), dma, dma,
        dma((4,)), dma((4,)), dma, dma,
    ]
    out = pl.pallas_call(
        kernel,
        out_shape=(
            jax.ShapeDtypeStruct((TOK, D), BF16),
            jax.ShapeDtypeStruct((1, TOK), BF16),
            jax.ShapeDtypeStruct((D // 16, FF), F32),
            jax.ShapeDtypeStruct((SLICE, D), F32),
        ),
        in_specs=[hbm, vmem, hbm, hbm, vmem, vmem, hbm],
        out_specs=(hbm, vmem, hbm, hbm),
        scratch_shapes=[pltpu.VMEM(shape, kind) for shape, kind in scratch] + semaphores,
        compiler_params=pltpu.CompilerParams(
            collective_id=0, has_side_effects=True, vmem_limit_bytes=56 * 1024 * 1024
        ),
        cost_estimate=pl.CostEstimate(flops=5 * 10**9, bytes_accessed=6 * 10**6, transcendentals=10**6),
    )(tokens, gain.reshape(1, D), w_in[0], w_out[0], expert_ids.reshape(1, TOK), gate, grad_out)
    out = pl.pallas_call(
        finish,
        out_shape=(
            jax.ShapeDtypeStruct((TOK, D), BF16),
            jax.ShapeDtypeStruct((TOK,), BF16),
            jax.ShapeDtypeStruct((D // 16, FF), F32),
            jax.ShapeDtypeStruct((SLICE, D), F32),
        ),
        in_specs=[vmem] * 4,
        out_specs=(vmem,) * 4,
    )(*out)
    return out[0], out[1], out[2][None], out[3][None]


def solution(mesh):
    placed = (
        P(("space", "dp"), None),
        P(),
        P("space", None, None),
        P("space", None, None),
        P(("space", "dp"), None),
        P(("space", "dp")),
        P(("space", "dp"), None),
    )
    return jax.shard_map(
        body,
        mesh=mesh,
        in_specs=placed,
        out_specs=(
            P(("space", "dp"), None),
            P(("space", "dp")),
            P("space", "dp", None),
            P("space", "dp", None),
        ),
        check_vma=False,
    )
```

```python
import functools

import jax
import jax.numpy as jnp
from jax import lax
from jax.experimental import pallas as pl
from jax.experimental.pallas import tpu as pltpu
from jax.sharding import PartitionSpec as P

MESH = pl.DeviceIdType.MESH
F32 = jnp.float32
BF16 = jnp.bfloat16
EPS = 1e-05
CAP = 24
TOK = 576
D = 512
FF = 1024
ROWS = 32 * CAP
SLICE = FF // 16


def coordinates():
    space, group = lax.axis_index("space"), lax.axis_index("dp")
    return space // 8, group // 4, ((space // 2) % 4) * 4 + group % 4, space % 2


def device(x, y, z, c):
    return {"space": (x * 4 + z // 4) * 2 + c, "dp": y * 4 + z % 4}


def nt(left, right):
    return lax.dot_general(left, right, (((1,), (1,)), ((), ())), preferred_element_type=F32)


def tn(left, right):
    return lax.dot_general(left, right, (((0,), (0,)), ((), ())), preferred_element_type=F32)


def nn(left, right):
    return lax.dot_general(left, right, (((1,), (0,)), ((), ())), preferred_element_type=F32)


def iota(shape, dim):
    return lax.broadcasted_iota(jnp.int32, shape, dim).astype(F32)


def kernel(
    tok_hbm, gain, win, wout, ids, gate, gout_hbm,
    gtok, ggate, gwin, gwout,
    tok, gout, blocks, wide, scaled_ref, col_ref, pair_ref, row_ref, sbuf, rbuf, xbuf, dbuf,
    wsend, wbuf, act_ref, gp_ref, dx_ref, gd_ref, gbuf, rl, rr,
    rt, bk, fsend, fout, mid_in, mid_out, pw, pout, gtok_v, gwin_v, gwout_v,
    tok_c, gout_c, wide_c, disp_s, disp_r, ret_s, ret_r, pre_s, pre_r, ag_s, ag_r, rl_s, rl_r, rr_s, rr_r, fin_s, fin_r, fo_s, fo_r,
    mi_s, mi_r, mo_s, mo_r,
):
    x, y, z, c = coordinates()
    zh, zl = z // 4, z % 4
    me = x * 8 + y * 2 + c
    group = y * 4 + zl
    home = y == zh
    right, left = device(x, y, (z + 1) % 16, c), device(x, y, (z + 15) % 16, c)
    away = jnp.logical_not(home)
    offset = (z + 16 - 4 * y) % 16

    into_tok = pltpu.make_async_copy(tok_hbm, tok, tok_c)
    into_gout = pltpu.make_async_copy(gout_hbm, gout, gout_c)
    into_tok.start()
    into_gout.start()

    def flip(v):
        return v + 1 - 2 * (v % 2)

    def slice_of(a, k):
        return ((a // 4 + 6 - k) % 4) * 4 + flip(a % 4)

    def plane_of(f, k):
        return ((f // 4 + 2 + k) % 4) * 4 + flip(f % 4)

    def block_in(n, a):
        return pltpu.make_async_copy(
            win.at[:, pl.ds(pl.multiple_of((a // 2) * 128, 128), 128)], blocks.at[n], wide_c.at[n]
        )

    def rows_in(n, a):
        return pltpu.make_async_copy(
            wout.at[pl.ds(pl.multiple_of(a * SLICE, SLICE), SLICE)], wsend.at[n, 1], wide_c.at[2 + n]
        )

    outer = (zl == 0) | (zl == 3)
    column = jnp.where(zl == 3, y + 4 - zh, y + 6 - zh) % 4
    reach = (jnp.where(column == 0, 4, column), jnp.where(column == 0, 8, column + 4))
    aims = [jnp.where(zl == 3, z + r, z + 16 - r) % 16 for r in reach]
    sends = [outer & (r <= 6) for r in reach]

    for n in range(2):
        @pl.when(sends[n])
        def _(n=n):
            block_in(n, slice_of(aims[n], zh)).start()
            rows_in(n, slice_of(aims[n], zh)).start()

    whole_in = pltpu.make_async_copy(win, wide, wide_c.at[4])

    def home_rows(f):
        return pltpu.make_async_copy(
            wout.at[pl.ds(pl.multiple_of(f * SLICE, SLICE), SLICE)], wbuf.at[plane_of(f, y), 1], wide_c.at[5 + f]
        )

    @pl.when(home)
    def _():
        whole_in.start()

        @pl.loop(0, 16)
        def _(f):
            home_rows(f).start()

    barrier = pltpu.get_barrier_semaphore()

    def greet(to):
        pl.semaphore_signal(barrier, inc=1, device_id=to, device_id_type=MESH)

    def peer(j):
        px, py, pc = (x + j // 8) % 4, (y + (j // 2) % 4) % 4, (c + j) % 2
        return device(px, py, z, pc), px * 8 + py * 2 + pc

    @pl.loop(1, 32)
    def _(j):
        greet(peer(j)[0])

    @pl.loop(1, 16)
    def _(j):
        greet(device(x, y, (z + j) % 16, c))

    near = jnp.where(offset < 10, offset - 3, 16 - offset)
    giver = jnp.where(
        offset < 10,
        device(x, (y + near) % 4, (4 * y + 3) % 16, c)["space"],
        device(x, (y + near + 2) % 4, 4 * y, c)["space"],
    )
    giver_group = jnp.where(offset < 10, ((y + near) % 4) * 4 + 3, ((y + near + 2) % 4) * 4)
    giver = {"space": giver, "dp": giver_group}

    @pl.when(away)
    def _():
        greet(giver)

    def gather(a, h, way):
        return pltpu.make_async_remote_copy(
            src_ref=wbuf.at[a, h], dst_ref=wbuf.at[a, h],
            send_sem=ag_s.at[way, a, h], recv_sem=ag_r.at[a, h],
            device_id=(right, left)[way], device_id_type=MESH,
        )

    def pre(n, h):
        return pltpu.make_async_remote_copy(
            src_ref=wsend.at[n, h], dst_ref=wbuf.at[aims[n], h], send_sem=pre_s.at[n, h], recv_sem=pre_r.at[h],
            device_id=device(x, zh, aims[n], c), device_id_type=MESH,
        )

    for n in range(2):
        @pl.when(sends[n])
        def _(n=n):
            block_in(n, slice_of(aims[n], zh)).wait()
            rows_in(n, slice_of(aims[n], zh)).wait()
            half = (slice_of(aims[n], zh) % 2).astype(F32)
            turned = blocks[n].astype(F32).T
            wsend[n, 0] = (turned[0:SLICE] * (1.0 - half) + turned[SLICE : 2 * SLICE] * half).astype(BF16)

    @pl.when(home)
    def _():
        whole_in.wait()
        for j in range(8):
            turned = wide[:, j * 128 : (j + 1) * 128].astype(F32).T.astype(BF16)
            wbuf[plane_of(2 * j, y), 0] = turned[0:SLICE]
            wbuf[plane_of(2 * j + 1, y), 0] = turned[SLICE : 2 * SLICE]

        @pl.loop(0, 16)
        def _(f):
            home_rows(f).wait()

    aimed = jnp.where(sends[0], 1, 0) + jnp.where(sends[1], 1, 0)
    pl.semaphore_wait(barrier, 46 + aimed)

    for h in range(2):
        for n in range(2):
            @pl.when(sends[n])
            def _(n=n, h=h):
                pre(n, h).start()

    @pl.when(home)
    def _():
        @pl.when(zl == 3)
        def _():
            @pl.loop(0, 8)
            def _(k):
                for h in range(2):
                    gather((z + 16 - k) % 16, h, 0).start()

        @pl.when(zl == 0)
        def _():
            @pl.loop(0, 7)
            def _(k):
                for h in range(2):
                    gather((z + k) % 16, h, 1).start()

    same = (iota((TOK, TOK), 0) == iota((TOK, TOK), 1)).astype(F32).astype(BF16)
    lines = jnp.where(iota((8, TOK), 0) == 0.0, ids[...].astype(F32), gate[...].astype(F32).reshape(1, TOK))
    columns = nt(same, lines.astype(BF16))
    expert, gate_col = columns[:, 0:1], columns[:, 1:2]
    onehot = (expert == iota((TOK, 128), 1)).astype(F32)
    earlier = (iota((TOK, TOK), 0) > iota((TOK, TOK), 1)).astype(F32).astype(BF16)
    before = nn(earlier, onehot.astype(BF16))
    clipped = jnp.minimum(before, float(CAP)) * onehot
    rank = jnp.sum(clipped, axis=1, keepdims=True)
    kept = rank < float(CAP)
    expert_row = ids[...].astype(F32)
    rank_row = nt(jnp.ones((8, 128), BF16), clipped.astype(BF16))
    row_ref[...] = jnp.where(rank_row < float(CAP), expert_row * float(CAP) + rank_row, -1.0)
    col_ref[...] = jnp.where(
        iota((TOK, 128), 1) == 0.0,
        expert,
        jnp.where(iota((TOK, 128), 1) == 1.0, rank, gate_col),
    )

    into_tok.wait()
    into_gout.wait()

    @pl.loop(0, 4)
    def _(i):
        at = pl.ds(pl.multiple_of(i * 144, 16), 144)
        values = tok[at, :].astype(F32)
        center = values - jnp.mean(values, axis=1, keepdims=True)
        spread = lax.rsqrt(jnp.mean(center * center, axis=1, keepdims=True) + EPS)
        scaled = center * spread
        scaled_ref[at, 0:D] = scaled
        scaled_ref[at, D : D + 128] = jnp.broadcast_to(spread, (144, 128))
        pair_ref[at, 0:D] = (scaled * gain[...]).astype(BF16)
        pair_ref[at, D : 2 * D] = (col_ref[at, 2:3] * gout[at, :].astype(F32)).astype(BF16)

    last_right, last_left = offset == 15, offset == 4

    def own_slice():
        for h in range(2):
            pltpu.make_async_remote_copy(
                src_ref=wsend.at[0, h], dst_ref=wbuf.at[z, h], send_sem=pre_s.at[0, h], recv_sem=pre_r.at[h],
                device_id=right, device_id_type=MESH,
            ).wait_recv()

            @pl.when(jnp.logical_not(last_right))
            def _(h=h):
                gather(z, h, 0).start()

            @pl.when(jnp.logical_not(last_left))
            def _(h=h):
                gather(z, h, 1).start()

    def hop(k):
        a, b = (z + 16 - k) % 16, (z + k) % 16

        @pl.when(away)
        def _():
            for h in range(2):
                gather(a, h, 0).wait_recv()

                @pl.when((k < 8) & jnp.logical_not(last_right))
                def _(h=h):
                    gather(a, h, 0).start()

                @pl.when(k < 8)
                def _(h=h):
                    gather(b, h, 1).wait_recv()

                @pl.when((k < 7) & jnp.logical_not(last_left))
                def _(h=h):
                    gather(b, h, 1).start()

    def dispatch(j):
        to, index = peer(j)
        return pltpu.make_async_remote_copy(
            src_ref=sbuf.at[index], dst_ref=rbuf.at[me], send_sem=disp_s.at[j], recv_sem=disp_r.at[j],
            device_id=to, device_id_type=MESH,
        )

    @pl.loop(0, 4)
    def _(i):
        dx = (2 + 3 * i) % 4
        first = ((x + dx) % 4) * 8
        slots = iota((8 * CAP, TOK), 0) + (first * CAP).astype(F32)
        chosen = (slots == row_ref[0:1, :]).astype(F32).astype(BF16)
        placed = nn(chosen, pair_ref[...])
        for e in range(8):
            rows = placed[e * CAP : (e + 1) * CAP]
            sbuf[first + e] = jnp.concatenate([rows[:, 0:D], rows[:, D : 2 * D]], axis=0).astype(BF16)

        @pl.loop(jnp.where(dx == 0, 1, 0), 8)
        def _(j):
            dispatch(dx * 8 + j).start()

    rbuf[me] = sbuf[me]

    @pl.when(away)
    def _():
        own_slice()

    @pl.loop(1, 5)
    def _(k):
        hop(k)

    @pl.loop(0, 16)
    def _(m):
        dx, dy = m // 4, m % 4
        for dc in range(2):
            @pl.when(m * 2 + dc > 0)
            def _(dc=dc):
                dispatch(m * 2 + dc).wait_recv()

        sx, sy = (x + 4 - dx) % 4, (y + 4 - dy) % 4
        n = sx * 4 + sy
        one, two = rbuf[n * 2].astype(F32), rbuf[n * 2 + 1].astype(F32)
        xbuf[n] = jnp.concatenate([one[0:CAP], two[0:CAP]], axis=0).astype(BF16)
        dbuf[n] = jnp.concatenate([one[CAP : 2 * CAP], two[CAP : 2 * CAP]], axis=0).astype(BF16)

    def reduce_left(s, h, src):
        return pltpu.make_async_remote_copy(
            src_ref=src.at[pl.ds(h * SLICE, SLICE)], dst_ref=rl.at[s, pl.ds(h * SLICE, SLICE)],
            send_sem=rl_s.at[s, h], recv_sem=rl_r.at[s, h], device_id=left, device_id_type=MESH,
        )

    def reduce_right(s, h, src):
        return pltpu.make_async_remote_copy(
            src_ref=src.at[pl.ds(h * SLICE, SLICE)], dst_ref=rr.at[s, pl.ds(h * SLICE, SLICE)],
            send_sem=rr_s.at[s, h], recv_sem=rr_r.at[s, h], device_id=right, device_id_type=MESH,
        )

    def reduce_step(s):
        for h in range(2):
            at = pl.ds(h * SLICE, SLICE)

            @pl.when(s == 0)
            def _(h=h):
                reduce_left(0, h, gbuf.at[0]).start()
                reduce_right(0, h, gbuf.at[1]).start()

            @pl.when(s > 0)
            def _(h=h, at=at):
                reduce_left(s - 1, h, gbuf.at[0]).wait_recv()
                rl[s - 1, at] = (rl[s - 1, at].astype(F32) + gbuf[2 * s, at].astype(F32)).astype(BF16)
                reduce_left(s, h, rl.at[s - 1]).start()

            @pl.when((s > 0) & (s < 7))
            def _(h=h, at=at):
                reduce_right(s - 1, h, gbuf.at[0]).wait_recv()
                rr[s - 1, at] = (rr[s - 1, at].astype(F32) + gbuf[2 * s + 1, at].astype(F32)).astype(BF16)
                reduce_right(s, h, rr.at[s - 1]).start()

    @pl.loop(0, 4)
    def _(g):
        held = [(z + 2 * g) % 16, (z + 15 - 2 * g) % 16, (z + 2 * g + 1) % 16, (z + 14 - 2 * g) % 16]
        w_in = jnp.concatenate([wbuf[a, 0] for a in held], axis=0)
        w_out = jnp.concatenate([wbuf[a, 1] for a in held], axis=0)

        @pl.loop(0, 4)
        def _(i):
            four = pl.ds(i * 4, 4)
            at = pl.ds(pl.multiple_of(i * 192, 16), 192)
            pre_act = nt(xbuf[four].reshape(192, D), w_in)
            grad_act = nt(dbuf[four].reshape(192, D), w_out)
            square = pre_act * pre_act
            curve = jnp.tanh(0.7978845608028654 * pre_act * (1.0 + 0.044715 * square))
            half_up = 0.5 * (1.0 + curve)
            activity = (pre_act * half_up).astype(BF16)
            slope = half_up + 0.5 * pre_act * (1.0 - curve * curve) * (
                0.7978845608028654 * (1.0 + 3 * 0.044715 * square)
            )
            grad_pre = (grad_act * slope).astype(BF16)
            act_ref[at, :] = activity
            gp_ref[at, :] = grad_pre
            dot = jnp.sum(activity.astype(F32) * grad_act, axis=1, keepdims=True)
            back = nn(grad_pre, w_in)

            @pl.when(g == 0)
            def _():
                gd_ref[at, :] = jnp.broadcast_to(dot, (192, 128))
                dx_ref[at, :] = back

            @pl.when(g > 0)
            def _():
                gd_ref[at, :] += jnp.broadcast_to(dot, (192, 128))
                dx_ref[at, :] += back

        part_in = tn(gp_ref[...], xbuf[...].reshape(ROWS, D)).astype(BF16)
        part_out = tn(act_ref[...], dbuf[...].reshape(ROWS, D)).astype(BF16)
        for j in range(4):
            gbuf[4 * g + j, 0:SLICE] = part_in[j * SLICE : (j + 1) * SLICE]
            gbuf[4 * g + j, SLICE : 2 * SLICE] = part_out[j * SLICE : (j + 1) * SLICE]

        @pl.when(g == 0)
        def _():
            reduce_step(0)

        @pl.when(g > 0)
        def _():
            reduce_step(2 * g - 1)

        @pl.when(g < 3)
        def _():
            hop(g + 5)

        @pl.when(g > 0)
        def _():
            reduce_step(2 * g)

        @pl.when(g == 2)
        def _():
            hop(8)

    place = iota((ROWS, 128), 0) - jnp.floor(iota((ROWS, 128), 0) * (1.0 / CAP) + 0.5 / CAP) * CAP
    lane = iota((ROWS, 128), 1)
    total = gd_ref[...]
    high = total.astype(BF16).astype(F32)
    spread_out = jnp.where(lane == place, high, jnp.where(lane == place + 32.0, total - high, 0.0)).astype(BF16)
    owner = iota((32, ROWS), 1) - iota((32, ROWS), 0) * CAP
    pick = ((owner >= 0.0) & (owner < float(CAP))).astype(F32).astype(BF16)
    gd_ref[0:32, :] = nn(pick, spread_out)

    def give_back(j):
        to, index = peer(j)
        return pltpu.make_async_remote_copy(
            src_ref=rt.at[index], dst_ref=bk.at[me], send_sem=ret_s.at[j], recv_sem=ret_r.at[j],
            device_id=to, device_id_type=MESH,
        )

    @pl.loop(0, 32)
    def _(j):
        index = peer(j)[1]
        rows = dx_ref[pl.ds(pl.multiple_of(index * CAP, 8), CAP), :]
        extra = jnp.broadcast_to(gd_ref[pl.ds(index, 1), :], (8, 128))
        extra = jnp.concatenate([extra, jnp.zeros((8, D - 128), F32)], axis=1)
        rt[index] = jnp.concatenate([rows, extra], axis=0).astype(BF16)

        @pl.when(j > 0)
        def _():
            give_back(j).start()

    bk[me] = rt[me]

    reduce_step(jnp.int32(7))

    owner = (zh + 4 - y) % 4

    def cross_in(p):
        return pltpu.make_async_remote_copy(
            src_ref=fsend.at[pl.ds(p * 4, 4)], dst_ref=mid_in.at[y], send_sem=mi_s.at[p], recv_sem=mi_r.at[y],
            device_id=device(x, p, z, c), device_id_type=MESH,
        )

    def crossed_in(k):
        return pltpu.make_async_remote_copy(
            src_ref=mid_in.at[k], dst_ref=mid_in.at[k], send_sem=mi_s.at[k], recv_sem=mi_r.at[k],
            device_id=right, device_id_type=MESH,
        )

    cross_out = pltpu.make_async_remote_copy(
        src_ref=fout, dst_ref=mid_out, send_sem=mo_s, recv_sem=mo_r,
        device_id=device(x, owner, z, c), device_id_type=MESH,
    )

    def summed(h):
        at = pl.ds(h * SLICE, SLICE)
        reduce_left(7, h, gbuf.at[0]).wait_recv()
        reduce_right(6, h, gbuf.at[0]).wait_recv()
        return rl[7, at].astype(F32) + rr[6, at].astype(F32) + gbuf[15, at].astype(F32)

    turned = summed(0).T.reshape(16, 32, SLICE)
    fsend[...] = jnp.concatenate([turned[:, 0:16], turned[:, 16:32]], axis=2).astype(BF16)

    @pl.loop(0, 4)
    def _(p):
        @pl.when(p != y)
        def _():
            cross_in(p).start()

        @pl.when(p == y)
        def _():
            mid_in[p] = fsend[pl.ds(p * 4, 4)]

    fout[...] = summed(1).astype(BF16)

    @pl.when(owner != y)
    def _():
        cross_out.start()

    @pl.when(owner == y)
    def _():
        mid_out[...] = fout[...]

    def keep_in(j):
        return pltpu.make_async_remote_copy(
            src_ref=mid_in.at[j // 4, j % 4], dst_ref=pw.at[z], send_sem=fin_s.at[j], recv_sem=fin_r.at[z],
            device_id=device(x, y, j, c), device_id_type=MESH,
        )

    def came_in(t):
        return pltpu.make_async_remote_copy(
            src_ref=pw.at[t], dst_ref=pw.at[t], send_sem=fin_s.at[t], recv_sem=fin_r.at[t],
            device_id=right, device_id_type=MESH,
        )

    keep_out = pltpu.make_async_remote_copy(
        src_ref=mid_out, dst_ref=pout, send_sem=fo_s, recv_sem=fo_r,
        device_id=device(x, y, owner * 4 + flip(zl), c), device_id_type=MESH,
    )

    @pl.when(owner != y)
    def _():
        cross_out.wait_recv()

    keep_out.start()

    @pl.loop(0, 16)
    def _(j):
        @pl.when((j % 4 == 0) & (j // 4 != y))
        def _():
            crossed_in(j // 4).wait_recv()

        @pl.when(j != z)
        def _():
            keep_in(j).start()

        @pl.when(j == z)
        def _():
            pw[z] = mid_in[zh, zl]

    out_tok = pltpu.make_async_copy(gtok_v, gtok, tok_c)
    out_win = pltpu.make_async_copy(gwin_v, gwin, gout_c)
    out_wout = pltpu.make_async_copy(gwout_v, gwout, wide_c.at[4])

    @pl.loop(1, 32)
    def _(j):
        give_back(j).wait_recv()

    @pl.loop(0, 3)
    def _(i):
        at = pl.ds(pl.multiple_of(i * 192, 16), 192)
        expert, rank = col_ref[at, 0:1], col_ref[at, 1:2]
        kept = rank < float(CAP)
        slot = iota((192, 1024), 1)
        returned = bk[...].reshape(1024, D)
        chosen = (slot == jnp.where(kept, expert * 32.0 + rank, -1.0)).astype(F32).astype(BF16)
        token_grad = nn(chosen, returned)
        line = (slot == expert * 32.0 + float(CAP)).astype(F32).astype(BF16)
        products = nn(line, returned[:, 0:128])
        lane = iota((192, 128), 1)
        product = jnp.sum(
            jnp.where((lane == rank) | (lane == rank + 32.0), products, 0.0), axis=1, keepdims=True
        )
        scaled, spread = scaled_ref[at, 0:D], scaled_ref[at, D : D + 1]
        u = token_grad * gain[...]
        mean = jnp.mean(u, axis=1, keepdims=True)
        cross = jnp.mean(u * scaled, axis=1, keepdims=True)
        branch = jnp.where(kept, spread * (u - mean - scaled * cross), 0.0)
        gtok_v[at, :] = (gout[at, :].astype(F32) + branch).astype(BF16)
        answer = jnp.where(kept, product / col_ref[at, 2:3], 0.0)
        top = answer.astype(BF16).astype(F32)
        col_ref[at, :] = jnp.where(lane == 0.0, top, jnp.where(lane == 1.0, answer - top, 0.0))

    ggate[...] = nt(jnp.ones((8, 128), BF16), col_ref[...].astype(BF16))[0:1, :].astype(BF16)

    out_tok.start()

    @pl.loop(1, 16)
    def _(j):
        came_in((z + j) % 16).wait_recv()

    for j in range(8):
        wide_rows = [
            pw[((f // 4 + zh) % 4) * 4 + flip(f % 4)].astype(F32) for f in (2 * j, 2 * j + 1)
        ]
        upper = jnp.concatenate([wide_rows[0][:, 0:SLICE], wide_rows[1][:, 0:SLICE]], axis=1)
        lower = jnp.concatenate([wide_rows[0][:, SLICE : 2 * SLICE], wide_rows[1][:, SLICE : 2 * SLICE]], axis=1)
        gwin_v[0:16, j * 128 : (j + 1) * 128] = upper
        gwin_v[16:32, j * 128 : (j + 1) * 128] = lower
    out_win.start()
    keep_out.wait_recv()
    gwout_v[...] = pout[...].astype(F32)
    out_wout.start()

    for n in range(2):
        @pl.when(sends[n])
        def _(n=n):
            pre(n, 0).wait_send()
            pre(n, 1).wait_send()

    @pl.loop(1, 32)
    def _(j):
        dispatch(j).wait_send()
        give_back(j).wait_send()

    @pl.loop(0, 8)
    def _(k):
        for h in range(2):
            @pl.when(((offset > 3) & jnp.logical_not(last_right)) | (offset == 3))
            def _(h=h):
                gather((z + 16 - k) % 16, h, 0).wait_send()

            @pl.when((k < 7) & (((offset > 3) & jnp.logical_not(last_left)) | (offset == 0)))
            def _(h=h):
                gather((z + k) % 16, h, 1).wait_send()

            reduce_left(k, h, gbuf.at[0]).wait_send()

            @pl.when(k < 7)
            def _(h=h):
                reduce_right(k, h, gbuf.at[0]).wait_send()

    @pl.loop(0, 16)
    def _(j):
        @pl.when(j != z)
        def _():
            keep_in(j).wait_send()

        @pl.when((j < 4) & (j != y))
        def _():
            cross_in(j).wait_send()

    @pl.when(owner != y)
    def _():
        cross_out.wait_send()

    keep_out.wait_send()
    out_tok.wait()
    out_win.wait()
    out_wout.wait()


def finish(tok, gate, win, wout, tok_out, gate_out, win_out, wout_out):
    tok_out[...] = tok[...]
    gate_out[...] = gate[0, :]
    win_out[...] = win[...]
    wout_out[...] = wout[...]


def body(tokens, gain, w_in, w_out, expert_ids, gate, grad_out):
    vmem = pl.BlockSpec(memory_space=pltpu.VMEM)
    hbm = pl.BlockSpec(memory_space=pl.ANY)
    dma = pltpu.SemaphoreType.DMA
    scratch = [
        ((TOK, D), BF16), ((TOK, D), BF16), ((2, D, 128), BF16), ((D, FF), BF16),
        ((TOK, D + 128), F32), ((TOK, 128), F32), ((TOK, 2 * D), BF16), ((8, TOK), F32),
        ((32, 2 * CAP, D), BF16), ((32, 2 * CAP, D), BF16), ((16, 2 * CAP, D), BF16), ((16, 2 * CAP, D), BF16),
        ((2, 2, SLICE, D), BF16), ((16, 2, SLICE, D), BF16), ((ROWS, 4 * SLICE), BF16), ((ROWS, 4 * SLICE), BF16),
        ((ROWS, D), F32), ((ROWS, 128), F32), ((16, 2 * SLICE, D), BF16),
        ((8, 2 * SLICE, D), BF16), ((7, 2 * SLICE, D), BF16),
        ((32, 32, D), BF16), ((32, 32, D), BF16), ((16, 16, 128), BF16), ((SLICE, D), BF16),
        ((4, 4, 16, 128), BF16), ((SLICE, D), BF16),
        ((16, 16, 128), BF16), ((SLICE, D), BF16), ((TOK, D), BF16), ((D // 16, FF), F32), ((SLICE, D), F32),
    ]
    semaphores = [
        dma, dma, dma((21,)),
        dma((32,)), dma((32,)), dma((32,)), dma((32,)), dma((2, 2)), dma((2,)), dma((2, 16, 2)), dma((16, 2)),
        dma((8, 2)), dma((8, 2)), dma((7, 2)), dma((7, 2)), dma((16,)), dma((16,)), dma, dma,
        dma((4,)), dma((4,)), dma, dma,
    ]
    out = pl.pallas_call(
        kernel,
        out_shape=(
            jax.ShapeDtypeStruct((TOK, D), BF16),
            jax.ShapeDtypeStruct((1, TOK), BF16),
            jax.ShapeDtypeStruct((D // 16, FF), F32),
            jax.ShapeDtypeStruct((SLICE, D), F32),
        ),
        in_specs=[hbm, vmem, hbm, hbm, vmem, vmem, hbm],
        out_specs=(hbm, vmem, hbm, hbm),
        scratch_shapes=[pltpu.VMEM(shape, kind) for shape, kind in scratch] + semaphores,
        compiler_params=pltpu.CompilerParams(
            collective_id=0, has_side_effects=True, vmem_limit_bytes=56 * 1024 * 1024
        ),
        cost_estimate=pl.CostEstimate(flops=5 * 10**9, bytes_accessed=6 * 10**6, transcendentals=10**6),
    )(tokens, gain.reshape(1, D), w_in[0], w_out[0], expert_ids.reshape(1, TOK), gate, grad_out)
    out = pl.pallas_call(
        finish,
        out_shape=(
            jax.ShapeDtypeStruct((TOK, D), BF16),
            jax.ShapeDtypeStruct((TOK,), BF16),
            jax.ShapeDtypeStruct((D // 16, FF), F32),
            jax.ShapeDtypeStruct((SLICE, D), F32),
        ),
        in_specs=[vmem] * 4,
        out_specs=(vmem,) * 4,
    )(*out)
    return out[0], out[1], out[2][None], out[3][None]


def solution(mesh):
    placed = (
        P(("space", "dp"), None),
        P(),
        P("space", None, None),
        P("space", None, None),
        P(("space", "dp"), None),
        P(("space", "dp")),
        P(("space", "dp"), None),
    )
    return jax.shard_map(
        body,
        mesh=mesh,
        in_specs=placed,
        out_specs=(
            P(("space", "dp"), None),
            P(("space", "dp")),
            P("space", "dp", None),
            P("space", "dp", None),
        ),
        check_vma=False,
    )
```

```python
import functools

import jax
import jax.numpy as jnp
from jax import lax
from jax.experimental import pallas as pl
from jax.experimental.pallas import tpu as pltpu
from jax.sharding import PartitionSpec as P

MESH = pl.DeviceIdType.MESH
F32 = jnp.float32
BF16 = jnp.bfloat16
EPS = 1e-05
CAP = 24
TOK = 576
D = 512
FF = 1024
ROWS = 32 * CAP
SLICE = FF // 16
PART = SLICE // 2


def coordinates():
    space, group = lax.axis_index("space"), lax.axis_index("dp")
    return space // 8, group // 4, ((space // 2) % 4) * 4 + group % 4, space % 2


def device(x, y, z, c):
    return {"space": (x * 4 + z // 4) * 2 + c, "dp": y * 4 + z % 4}


def nt(left, right):
    return lax.dot_general(left, right, (((1,), (1,)), ((), ())), preferred_element_type=F32)


def tn(left, right):
    return lax.dot_general(left, right, (((0,), (0,)), ((), ())), preferred_element_type=F32)


def nn(left, right):
    return lax.dot_general(left, right, (((1,), (0,)), ((), ())), preferred_element_type=F32)


def iota(shape, dim):
    return lax.broadcasted_iota(jnp.int32, shape, dim).astype(F32)


def kernel(
    tok_hbm, gain, win, wout, ids, gate, gout_hbm,
    gtok, ggate, gwin, gwout,
    tok, gout, blocks, wide, scaled_ref, col_ref, pair_ref, row_ref, sbuf, rbuf, xbuf, dbuf,
    wsend, wbuf, act_ref, gp_ref, dx_ref, gd_ref, gbuf, rl, rr,
    rt, bk, fsend, fout, mid_in, mid_out, pw, pout, gtok_v, gwin_v, gwout_v,
    tok_c, gout_c, wide_c, disp_s, disp_r, ret_s, ret_r, pre_s, pre_r, ag_s, ag_r, rl_s, rl_r, rr_s, rr_r, fin_s, fin_r, fo_s, fo_r,
    mi_s, mi_r, mo_s, mo_r,
):
    x, y, z, c = coordinates()
    zh, zl = z // 4, z % 4
    me = x * 8 + y * 2 + c
    group = y * 4 + zl
    home = y == zh
    right, left = device(x, y, (z + 1) % 16, c), device(x, y, (z + 15) % 16, c)
    away = jnp.logical_not(home)
    offset = (z + 16 - 4 * y) % 16

    into_tok = pltpu.make_async_copy(tok_hbm, tok, tok_c)
    into_gout = pltpu.make_async_copy(gout_hbm, gout, gout_c)
    into_tok.start()
    into_gout.start()

    def flip(v):
        return v + 1 - 2 * (v % 2)

    def slice_of(a, k):
        return ((a // 4 + 6 - k) % 4) * 4 + flip(a % 4)

    def plane_of(f, k):
        return ((f // 4 + 2 + k) % 4) * 4 + flip(f % 4)

    def block_in(n, a):
        return pltpu.make_async_copy(
            win.at[:, pl.ds(pl.multiple_of((a // 2) * 128, 128), 128)], blocks.at[n], wide_c.at[n]
        )

    def rows_in(n, a):
        return pltpu.make_async_copy(
            wout.at[pl.ds(pl.multiple_of(a * SLICE, SLICE), SLICE)], wsend.at[n, 1], wide_c.at[2 + n]
        )

    outer = (zl == 0) | (zl == 3)
    column = jnp.where(zl == 3, y + 4 - zh, y + 6 - zh) % 4
    reach = (jnp.where(column == 0, 4, column), jnp.where(column == 0, 8, column + 4))
    aims = [jnp.where(zl == 3, z + r, z + 16 - r) % 16 for r in reach]
    sends = [outer & (r <= 6) for r in reach]

    for n in range(2):
        @pl.when(sends[n])
        def _(n=n):
            block_in(n, slice_of(aims[n], zh)).start()
            rows_in(n, slice_of(aims[n], zh)).start()

    whole_in = pltpu.make_async_copy(win, wide, wide_c.at[4])

    def home_rows(f):
        return pltpu.make_async_copy(
            wout.at[pl.ds(pl.multiple_of(f * SLICE, SLICE), SLICE)], wbuf.at[plane_of(f, y), 1], wide_c.at[5 + f]
        )

    @pl.when(home)
    def _():
        whole_in.start()

        @pl.loop(0, 16)
        def _(f):
            home_rows(f).start()

    barrier = pltpu.get_barrier_semaphore()

    def greet(to):
        pl.semaphore_signal(barrier, inc=1, device_id=to, device_id_type=MESH)

    def peer(j):
        px, py, pc = (x + j // 8) % 4, (y + (j // 2) % 4) % 4, (c + j) % 2
        return device(px, py, z, pc), px * 8 + py * 2 + pc

    @pl.loop(1, 32)
    def _(j):
        greet(peer(j)[0])

    @pl.loop(1, 16)
    def _(j):
        greet(device(x, y, (z + j) % 16, c))

    near = jnp.where(offset < 10, offset - 3, 16 - offset)
    giver = jnp.where(
        offset < 10,
        device(x, (y + near) % 4, (4 * y + 3) % 16, c)["space"],
        device(x, (y + near + 2) % 4, 4 * y, c)["space"],
    )
    giver_group = jnp.where(offset < 10, ((y + near) % 4) * 4 + 3, ((y + near + 2) % 4) * 4)
    giver = {"space": giver, "dp": giver_group}

    @pl.when(away)
    def _():
        greet(giver)

    def gather(a, h, way):
        return pltpu.make_async_remote_copy(
            src_ref=wbuf.at[a, h], dst_ref=wbuf.at[a, h],
            send_sem=ag_s.at[way, a, h], recv_sem=ag_r.at[a, h],
            device_id=(right, left)[way], device_id_type=MESH,
        )

    def pre(n, h):
        return pltpu.make_async_remote_copy(
            src_ref=wsend.at[n, h], dst_ref=wbuf.at[aims[n], h], send_sem=pre_s.at[n, h], recv_sem=pre_r.at[h],
            device_id=device(x, zh, aims[n], c), device_id_type=MESH,
        )

    for n in range(2):
        @pl.when(sends[n])
        def _(n=n):
            block_in(n, slice_of(aims[n], zh)).wait()
            rows_in(n, slice_of(aims[n], zh)).wait()
            half = (slice_of(aims[n], zh) % 2).astype(F32)
            turned = blocks[n].T.astype(F32)
            wsend[n, 0] = (turned[0:SLICE] * (1.0 - half) + turned[SLICE : 2 * SLICE] * half).astype(BF16)

    @pl.when(home)
    def _():
        whole_in.wait()
        for j in range(8):
            turned = wide[:, j * 128 : (j + 1) * 128].T
            wbuf[plane_of(2 * j, y), 0] = turned[0:SLICE]
            wbuf[plane_of(2 * j + 1, y), 0] = turned[SLICE : 2 * SLICE]

        @pl.loop(0, 16)
        def _(f):
            home_rows(f).wait()

    aimed = jnp.where(sends[0], 1, 0) + jnp.where(sends[1], 1, 0)
    pl.semaphore_wait(barrier, 46 + aimed)

    for h in range(2):
        for n in range(2):
            @pl.when(sends[n])
            def _(n=n, h=h):
                pre(n, h).start()

    @pl.when(home)
    def _():
        @pl.when(zl == 3)
        def _():
            @pl.loop(0, 8)
            def _(k):
                for h in range(2):
                    gather((z + 16 - k) % 16, h, 0).start()

        @pl.when(zl == 0)
        def _():
            @pl.loop(0, 7)
            def _(k):
                for h in range(2):
                    gather((z + k) % 16, h, 1).start()

    same = (iota((TOK, TOK), 0) == iota((TOK, TOK), 1)).astype(F32).astype(BF16)
    lines = jnp.where(iota((8, TOK), 0) == 0.0, ids[...].astype(F32), gate[...].astype(F32).reshape(1, TOK))
    columns = nt(same, lines.astype(BF16))
    expert, gate_col = columns[:, 0:1], columns[:, 1:2]
    onehot = (expert == iota((TOK, 128), 1)).astype(F32)
    earlier = (iota((TOK, TOK), 0) > iota((TOK, TOK), 1)).astype(F32).astype(BF16)
    before = nn(earlier, onehot.astype(BF16))
    clipped = jnp.minimum(before, float(CAP)) * onehot
    rank = jnp.sum(clipped, axis=1, keepdims=True)
    kept = rank < float(CAP)
    expert_row = ids[...].astype(F32)
    rank_row = nt(jnp.ones((8, 128), BF16), clipped.astype(BF16))
    row_ref[...] = jnp.where(rank_row < float(CAP), expert_row * float(CAP) + rank_row, -1.0)
    col_ref[...] = jnp.where(
        iota((TOK, 128), 1) == 0.0,
        expert,
        jnp.where(iota((TOK, 128), 1) == 1.0, rank, gate_col),
    )

    into_tok.wait()
    into_gout.wait()

    @pl.loop(0, 4)
    def _(i):
        at = pl.ds(pl.multiple_of(i * 144, 16), 144)
        values = tok[at, :].astype(F32)
        center = values - jnp.mean(values, axis=1, keepdims=True)
        spread = lax.rsqrt(jnp.mean(center * center, axis=1, keepdims=True) + EPS)
        scaled = center * spread
        scaled_ref[at, 0:D] = scaled
        scaled_ref[at, D : D + 128] = jnp.broadcast_to(spread, (144, 128))
        pair_ref[at, 0:D] = (scaled * gain[...]).astype(BF16)
        pair_ref[at, D : 2 * D] = (col_ref[at, 2:3] * gout[at, :].astype(F32)).astype(BF16)

    last_right, last_left = offset == 15, offset == 4

    def own_slice():
        for h in range(2):
            pltpu.make_async_remote_copy(
                src_ref=wsend.at[0, h], dst_ref=wbuf.at[z, h], send_sem=pre_s.at[0, h], recv_sem=pre_r.at[h],
                device_id=right, device_id_type=MESH,
            ).wait_recv()

            @pl.when(jnp.logical_not(last_right))
            def _(h=h):
                gather(z, h, 0).start()

            @pl.when(jnp.logical_not(last_left))
            def _(h=h):
                gather(z, h, 1).start()

    def hop(k):
        a, b = (z + 16 - k) % 16, (z + k) % 16

        @pl.when(away)
        def _():
            for h in range(2):
                gather(a, h, 0).wait_recv()

                @pl.when((k < 8) & jnp.logical_not(last_right))
                def _(h=h):
                    gather(a, h, 0).start()

                @pl.when(k < 8)
                def _(h=h):
                    gather(b, h, 1).wait_recv()

                @pl.when((k < 7) & jnp.logical_not(last_left))
                def _(h=h):
                    gather(b, h, 1).start()

    def dispatch(j):
        to, index = peer(j)
        return pltpu.make_async_remote_copy(
            src_ref=sbuf.at[index], dst_ref=rbuf.at[me], send_sem=disp_s.at[j], recv_sem=disp_r.at[j],
            device_id=to, device_id_type=MESH,
        )

    @pl.loop(0, 4)
    def _(i):
        dx = (2 + 3 * i) % 4
        first = ((x + dx) % 4) * 8
        slots = iota((8 * CAP, TOK), 0) + (first * CAP).astype(F32)
        chosen = (slots == row_ref[0:1, :]).astype(F32).astype(BF16)
        placed = nn(chosen, pair_ref[...])
        for e in range(8):
            rows = placed[e * CAP : (e + 1) * CAP]
            sbuf[first + e] = jnp.concatenate([rows[:, 0:D], rows[:, D : 2 * D]], axis=0).astype(BF16)

        @pl.loop(jnp.where(dx == 0, 1, 0), 8)
        def _(j):
            dispatch(dx * 8 + j).start()

    rbuf[me] = sbuf[me]

    @pl.when(away)
    def _():
        own_slice()

    @pl.loop(1, 5)
    def _(k):
        hop(k)

    @pl.loop(0, 16)
    def _(m):
        dx, dy = m // 4, m % 4
        for dc in range(2):
            @pl.when(m * 2 + dc > 0)
            def _(dc=dc):
                dispatch(m * 2 + dc).wait_recv()

        sx, sy = (x + 4 - dx) % 4, (y + 4 - dy) % 4
        n = sx * 4 + sy
        one, two = rbuf[n * 2].astype(F32), rbuf[n * 2 + 1].astype(F32)
        xbuf[n] = jnp.concatenate([one[0:CAP], two[0:CAP]], axis=0).astype(BF16)
        dbuf[n] = jnp.concatenate([one[CAP : 2 * CAP], two[CAP : 2 * CAP]], axis=0).astype(BF16)

    def reduce_left(s, h, src):
        return pltpu.make_async_remote_copy(
            src_ref=src.at[pl.ds(h * PART, PART)], dst_ref=rl.at[s, pl.ds(h * PART, PART)],
            send_sem=rl_s.at[s, h], recv_sem=rl_r.at[s, h], device_id=left, device_id_type=MESH,
        )

    def reduce_right(s, h, src):
        return pltpu.make_async_remote_copy(
            src_ref=src.at[pl.ds(h * PART, PART)], dst_ref=rr.at[s, pl.ds(h * PART, PART)],
            send_sem=rr_s.at[s, h], recv_sem=rr_r.at[s, h], device_id=right, device_id_type=MESH,
        )

    def reduce_step(s):
        for h in range(4):
            at = pl.ds(h * PART, PART)

            @pl.when(s == 0)
            def _(h=h):
                reduce_left(0, h, gbuf.at[0]).start()
                reduce_right(0, h, gbuf.at[1]).start()

            @pl.when(s > 0)
            def _(h=h, at=at):
                reduce_left(s - 1, h, gbuf.at[0]).wait_recv()
                rl[s - 1, at] = (rl[s - 1, at].astype(F32) + gbuf[2 * s, at].astype(F32)).astype(BF16)
                reduce_left(s, h, rl.at[s - 1]).start()

            @pl.when((s > 0) & (s < 7))
            def _(h=h, at=at):
                reduce_right(s - 1, h, gbuf.at[0]).wait_recv()
                rr[s - 1, at] = (rr[s - 1, at].astype(F32) + gbuf[2 * s + 1, at].astype(F32)).astype(BF16)
                reduce_right(s, h, rr.at[s - 1]).start()

    @pl.loop(0, 4)
    def _(g):
        held = [(z + 2 * g) % 16, (z + 15 - 2 * g) % 16, (z + 2 * g + 1) % 16, (z + 14 - 2 * g) % 16]
        w_in = jnp.concatenate([wbuf[a, 0] for a in held], axis=0)
        w_out = jnp.concatenate([wbuf[a, 1] for a in held], axis=0)

        @pl.loop(0, 4)
        def _(i):
            four = pl.ds(i * 4, 4)
            at = pl.ds(pl.multiple_of(i * 192, 16), 192)
            pre_act = nt(xbuf[four].reshape(192, D), w_in)
            grad_act = nt(dbuf[four].reshape(192, D), w_out)
            square = pre_act * pre_act
            curve = jnp.tanh(0.7978845608028654 * pre_act * (1.0 + 0.044715 * square))
            half_up = 0.5 * (1.0 + curve)
            activity = (pre_act * half_up).astype(BF16)
            slope = half_up + 0.5 * pre_act * (1.0 - curve * curve) * (
                0.7978845608028654 * (1.0 + 3 * 0.044715 * square)
            )
            grad_pre = (grad_act * slope).astype(BF16)
            act_ref[at, :] = activity
            gp_ref[at, :] = grad_pre
            dot = jnp.sum(activity.astype(F32) * grad_act, axis=1, keepdims=True)
            back = nn(grad_pre, w_in)

            @pl.when(g == 0)
            def _():
                gd_ref[at, :] = jnp.broadcast_to(dot, (192, 128))
                dx_ref[at, :] = back

            @pl.when(g > 0)
            def _():
                gd_ref[at, :] += jnp.broadcast_to(dot, (192, 128))
                dx_ref[at, :] += back

        part_in = tn(gp_ref[...], xbuf[...].reshape(ROWS, D)).astype(BF16)
        part_out = tn(act_ref[...], dbuf[...].reshape(ROWS, D)).astype(BF16)
        for j in range(4):
            gbuf[4 * g + j, 0:SLICE] = part_in[j * SLICE : (j + 1) * SLICE]
            gbuf[4 * g + j, SLICE : 2 * SLICE] = part_out[j * SLICE : (j + 1) * SLICE]

        @pl.when(g == 0)
        def _():
            reduce_step(0)

        @pl.when(g > 0)
        def _():
            reduce_step(2 * g - 1)

        @pl.when(g < 3)
        def _():
            hop(g + 5)

        @pl.when(g > 0)
        def _():
            reduce_step(2 * g)

        @pl.when(g == 2)
        def _():
            hop(8)

    place = iota((ROWS, 128), 0) - jnp.floor(iota((ROWS, 128), 0) * (1.0 / CAP) + 0.5 / CAP) * CAP
    lane = iota((ROWS, 128), 1)
    total = gd_ref[...]
    high = total.astype(BF16).astype(F32)
    spread_out = jnp.where(lane == place, high, jnp.where(lane == place + 32.0, total - high, 0.0)).astype(BF16)
    owner = iota((32, ROWS), 1) - iota((32, ROWS), 0) * CAP
    pick = ((owner >= 0.0) & (owner < float(CAP))).astype(F32).astype(BF16)
    gd_ref[0:32, :] = nn(pick, spread_out)

    def give_back(j):
        to, index = peer(j)
        return pltpu.make_async_remote_copy(
            src_ref=rt.at[index], dst_ref=bk.at[me], send_sem=ret_s.at[j], recv_sem=ret_r.at[j],
            device_id=to, device_id_type=MESH,
        )

    @pl.loop(0, 32)
    def _(j):
        index = peer(j)[1]
        rows = dx_ref[pl.ds(pl.multiple_of(index * CAP, 8), CAP), :]
        extra = jnp.broadcast_to(gd_ref[pl.ds(index, 1), :], (8, 128))
        extra = jnp.concatenate([extra, jnp.zeros((8, D - 128), F32)], axis=1)
        rt[index] = jnp.concatenate([rows, extra], axis=0).astype(BF16)

        @pl.when(j > 0)
        def _():
            give_back(j).start()

    bk[me] = rt[me]

    reduce_step(jnp.int32(7))

    owner = (zh + 4 - y) % 4

    def cross_in(p):
        return pltpu.make_async_remote_copy(
            src_ref=fsend.at[pl.ds(p * 4, 4)], dst_ref=mid_in.at[y], send_sem=mi_s.at[p], recv_sem=mi_r.at[y],
            device_id=device(x, p, z, c), device_id_type=MESH,
        )

    def crossed_in(k):
        return pltpu.make_async_remote_copy(
            src_ref=mid_in.at[k], dst_ref=mid_in.at[k], send_sem=mi_s.at[k], recv_sem=mi_r.at[k],
            device_id=right, device_id_type=MESH,
        )

    cross_out = pltpu.make_async_remote_copy(
        src_ref=fout, dst_ref=mid_out, send_sem=mo_s, recv_sem=mo_r,
        device_id=device(x, owner, z, c), device_id_type=MESH,
    )

    def summed(h):
        at = pl.ds(h * SLICE, SLICE)
        for part in (2 * h, 2 * h + 1):
            reduce_left(7, part, gbuf.at[0]).wait_recv()
            reduce_right(6, part, gbuf.at[0]).wait_recv()
        return rl[7, at].astype(F32) + rr[6, at].astype(F32) + gbuf[15, at].astype(F32)

    turned = summed(0).T.reshape(16, 32, SLICE)
    fsend[...] = jnp.concatenate([turned[:, 0:16], turned[:, 16:32]], axis=2).astype(BF16)

    @pl.loop(0, 4)
    def _(p):
        @pl.when(p != y)
        def _():
            cross_in(p).start()

        @pl.when(p == y)
        def _():
            mid_in[p] = fsend[pl.ds(p * 4, 4)]

    fout[...] = summed(1).astype(BF16)

    @pl.when(owner != y)
    def _():
        cross_out.start()

    @pl.when(owner == y)
    def _():
        mid_out[...] = fout[...]

    def keep_in(j):
        return pltpu.make_async_remote_copy(
            src_ref=mid_in.at[j // 4, j % 4], dst_ref=pw.at[z], send_sem=fin_s.at[j], recv_sem=fin_r.at[z],
            device_id=device(x, y, j, c), device_id_type=MESH,
        )

    def came_in(t):
        return pltpu.make_async_remote_copy(
            src_ref=pw.at[t], dst_ref=pw.at[t], send_sem=fin_s.at[t], recv_sem=fin_r.at[t],
            device_id=right, device_id_type=MESH,
        )

    keep_out = pltpu.make_async_remote_copy(
        src_ref=mid_out, dst_ref=pout, send_sem=fo_s, recv_sem=fo_r,
        device_id=device(x, y, owner * 4 + flip(zl), c), device_id_type=MESH,
    )

    @pl.when(owner != y)
    def _():
        cross_out.wait_recv()

    keep_out.start()

    @pl.loop(0, 16)
    def _(j):
        @pl.when((j % 4 == 0) & (j // 4 != y))
        def _():
            crossed_in(j // 4).wait_recv()

        @pl.when(j != z)
        def _():
            keep_in(j).start()

        @pl.when(j == z)
        def _():
            pw[z] = mid_in[zh, zl]

    out_tok = pltpu.make_async_copy(gtok_v, gtok, tok_c)
    out_win = pltpu.make_async_copy(gwin_v, gwin, gout_c)
    out_wout = pltpu.make_async_copy(gwout_v, gwout, wide_c.at[4])

    @pl.loop(1, 32)
    def _(j):
        give_back(j).wait_recv()

    @pl.loop(0, 3)
    def _(i):
        at = pl.ds(pl.multiple_of(i * 192, 16), 192)
        expert, rank = col_ref[at, 0:1], col_ref[at, 1:2]
        kept = rank < float(CAP)
        slot = iota((192, 1024), 1)
        returned = bk[...].reshape(1024, D)
        chosen = (slot == jnp.where(kept, expert * 32.0 + rank, -1.0)).astype(F32).astype(BF16)
        token_grad = nn(chosen, returned)
        line = (slot == expert * 32.0 + float(CAP)).astype(F32).astype(BF16)
        products = nn(line, returned[:, 0:128])
        lane = iota((192, 128), 1)
        product = jnp.sum(
            jnp.where((lane == rank) | (lane == rank + 32.0), products, 0.0), axis=1, keepdims=True
        )
        scaled, spread = scaled_ref[at, 0:D], scaled_ref[at, D : D + 1]
        u = token_grad * gain[...]
        mean = jnp.mean(u, axis=1, keepdims=True)
        cross = jnp.mean(u * scaled, axis=1, keepdims=True)
        branch = jnp.where(kept, spread * (u - mean - scaled * cross), 0.0)
        gtok_v[at, :] = (gout[at, :].astype(F32) + branch).astype(BF16)
        answer = jnp.where(kept, product / col_ref[at, 2:3], 0.0)
        top = answer.astype(BF16).astype(F32)
        col_ref[at, :] = jnp.where(lane == 0.0, top, jnp.where(lane == 1.0, answer - top, 0.0))

    ggate[...] = nt(jnp.ones((8, 128), BF16), col_ref[...].astype(BF16))[0:1, :].astype(BF16)

    out_tok.start()

    @pl.loop(1, 16)
    def _(j):
        came_in((z + j) % 16).wait_recv()

    for j in range(8):
        wide_rows = [
            pw[((f // 4 + zh) % 4) * 4 + flip(f % 4)].astype(F32) for f in (2 * j, 2 * j + 1)
        ]
        upper = jnp.concatenate([wide_rows[0][:, 0:SLICE], wide_rows[1][:, 0:SLICE]], axis=1)
        lower = jnp.concatenate([wide_rows[0][:, SLICE : 2 * SLICE], wide_rows[1][:, SLICE : 2 * SLICE]], axis=1)
        gwin_v[0:16, j * 128 : (j + 1) * 128] = upper
        gwin_v[16:32, j * 128 : (j + 1) * 128] = lower
    out_win.start()
    keep_out.wait_recv()
    gwout_v[...] = pout[...].astype(F32)
    out_wout.start()

    for n in range(2):
        @pl.when(sends[n])
        def _(n=n):
            pre(n, 0).wait_send()
            pre(n, 1).wait_send()

    @pl.loop(1, 32)
    def _(j):
        dispatch(j).wait_send()
        give_back(j).wait_send()

    @pl.loop(0, 8)
    def _(k):
        for h in range(2):
            @pl.when(((offset > 3) & jnp.logical_not(last_right)) | (offset == 3))
            def _(h=h):
                gather((z + 16 - k) % 16, h, 0).wait_send()

            @pl.when((k < 7) & (((offset > 3) & jnp.logical_not(last_left)) | (offset == 0)))
            def _(h=h):
                gather((z + k) % 16, h, 1).wait_send()

            for part in (2 * h, 2 * h + 1):
                reduce_left(k, part, gbuf.at[0]).wait_send()

                @pl.when(k < 7)
                def _(part=part):
                    reduce_right(k, part, gbuf.at[0]).wait_send()

    @pl.loop(0, 16)
    def _(j):
        @pl.when(j != z)
        def _():
            keep_in(j).wait_send()

        @pl.when((j < 4) & (j != y))
        def _():
            cross_in(j).wait_send()

    @pl.when(owner != y)
    def _():
        cross_out.wait_send()

    keep_out.wait_send()
    out_tok.wait()
    out_win.wait()
    out_wout.wait()


def finish(tok, gate, win, wout, tok_out, gate_out, win_out, wout_out):
    tok_out[...] = tok[...]
    gate_out[...] = gate[0, :]
    win_out[...] = win[...]
    wout_out[...] = wout[...]


def body(tokens, gain, w_in, w_out, expert_ids, gate, grad_out):
    vmem = pl.BlockSpec(memory_space=pltpu.VMEM)
    hbm = pl.BlockSpec(memory_space=pl.ANY)
    dma = pltpu.SemaphoreType.DMA
    scratch = [
        ((TOK, D), BF16), ((TOK, D), BF16), ((2, D, 128), BF16), ((D, FF), BF16),
        ((TOK, D + 128), F32), ((TOK, 128), F32), ((TOK, 2 * D), BF16), ((8, TOK), F32),
        ((32, 2 * CAP, D), BF16), ((32, 2 * CAP, D), BF16), ((16, 2 * CAP, D), BF16), ((16, 2 * CAP, D), BF16),
        ((2, 2, SLICE, D), BF16), ((16, 2, SLICE, D), BF16), ((ROWS, 4 * SLICE), BF16), ((ROWS, 4 * SLICE), BF16),
        ((ROWS, D), F32), ((ROWS, 128), F32), ((16, 2 * SLICE, D), BF16),
        ((8, 2 * SLICE, D), BF16), ((7, 2 * SLICE, D), BF16),
        ((32, 32, D), BF16), ((32, 32, D), BF16), ((16, 16, 128), BF16), ((SLICE, D), BF16),
        ((4, 4, 16, 128), BF16), ((SLICE, D), BF16),
        ((16, 16, 128), BF16), ((SLICE, D), BF16), ((TOK, D), BF16), ((D // 16, FF), F32), ((SLICE, D), F32),
    ]
    semaphores = [
        dma, dma, dma((21,)),
        dma((32,)), dma((32,)), dma((32,)), dma((32,)), dma((2, 2)), dma((2,)), dma((2, 16, 2)), dma((16, 2)),
        dma((8, 4)), dma((8, 4)), dma((7, 4)), dma((7, 4)), dma((16,)), dma((16,)), dma, dma,
        dma((4,)), dma((4,)), dma, dma,
    ]
    out = pl.pallas_call(
        kernel,
        out_shape=(
            jax.ShapeDtypeStruct((TOK, D), BF16),
            jax.ShapeDtypeStruct((1, TOK), BF16),
            jax.ShapeDtypeStruct((D // 16, FF), F32),
            jax.ShapeDtypeStruct((SLICE, D), F32),
        ),
        in_specs=[hbm, vmem, hbm, hbm, vmem, vmem, hbm],
        out_specs=(hbm, vmem, hbm, hbm),
        scratch_shapes=[pltpu.VMEM(shape, kind) for shape, kind in scratch] + semaphores,
        compiler_params=pltpu.CompilerParams(
            collective_id=0, has_side_effects=True, vmem_limit_bytes=56 * 1024 * 1024
        ),
        cost_estimate=pl.CostEstimate(flops=5 * 10**9, bytes_accessed=6 * 10**6, transcendentals=10**6),
    )(tokens, gain.reshape(1, D), w_in[0], w_out[0], expert_ids.reshape(1, TOK), gate, grad_out)
    out = pl.pallas_call(
        finish,
        out_shape=(
            jax.ShapeDtypeStruct((TOK, D), BF16),
            jax.ShapeDtypeStruct((TOK,), BF16),
            jax.ShapeDtypeStruct((D // 16, FF), F32),
            jax.ShapeDtypeStruct((SLICE, D), F32),
        ),
        in_specs=[vmem] * 4,
        out_specs=(vmem,) * 4,
    )(*out)
    return out[0], out[1], out[2][None], out[3][None]


def solution(mesh):
    placed = (
        P(("space", "dp"), None),
        P(),
        P("space", None, None),
        P("space", None, None),
        P(("space", "dp"), None),
        P(("space", "dp")),
        P(("space", "dp"), None),
    )
    return jax.shard_map(
        body,
        mesh=mesh,
        in_specs=placed,
        out_specs=(
            P(("space", "dp"), None),
            P(("space", "dp")),
            P("space", "dp", None),
            P("space", "dp", None),
        ),
        check_vma=False,
    )
```
